512 devices in a mesh: seq: 128 (over y, z, core), fsdp: 4 (over x).
Axes of the slice: x: 4, y: 4, z: 16, core: 2. Of those that a mesh axis runs over, the one named last changes fastest.
Arguments:
- queries: bfloat16 [16384, 4096], P('seq', 'fsdp'), may hold values from -6 to 6
- keys: bfloat16 [16384, 4096], P('seq', 'fsdp'), may hold values from -6 to 6
- values: bfloat16 [16384, 4096], P('seq', 'fsdp'), may hold values from -6 to 6
- grad_out: bfloat16 [16384, 4096], P('seq', 'fsdp'), may hold values from -16 to 16
- norm_gain: float32 [4096], P('fsdp'), may hold values from 0.3 to 20
- norm_bias: float32 [4096], P('fsdp'), may hold values from -8 to 8
- first_moment: float32 [2, 4096], P(None, 'fsdp'), may hold values from -500 to 500
- second_moment: float32 [2, 4096], P(None, 'fsdp'), may hold values from 10000 to 1000000
Outputs:
- grad_queries: bfloat16 [16384, 4096], P('seq', 'fsdp')
- grad_keys: bfloat16 [16384, 4096], P('seq', 'fsdp')
- grad_values: bfloat16 [16384, 4096], P('seq', 'fsdp')
- new_gain: float32 [4096], P('fsdp')
- new_bias: float32 [4096], P('fsdp')
The draws below stay inside these ranges and needn't reach their ends.
All inputs are finite; a program needn't handle non-finite values.
Results may differ from the reference program's by a relative error of at most 0.0075.
Values sent between devices are 32-bit elements; how exact they have to be, the bound alone decides.
No kernel may reach another device: no remote copies, remote signals or barrier semaphores. Data moves between devices by JAX's collectives and lax.ppermute only.
A program may use at most 192 MiB of HBM per device.

```python
import jax
import jax.numpy as jnp
from jax import lax

HEADS = 32
HEAD_DIM = 128
SPAN = 128
TOKENS = 16384
CHANNELS = 4096


def ramp(count, power):
    position = jnp.arange(count, dtype=jnp.float32) / (count - 1)
    return (1.0 + 2.0 * position) ** power


def draw_grad_out(key, part):
    key = jax.random.fold_in(key, 11)
    shape = (TOKENS, HEADS * HEAD_DIM)
    base = jnp.clip(jax.random.normal(key, shape, jnp.float32), -4.0, 4.0)
    scale = ramp(TOKENS, 1.0)
    return (base * scale[:, None]).astype(jnp.bfloat16)


def draw_norm_gain(key, part):
    key = jax.random.fold_in(key, 12)
    count = HEADS * HEAD_DIM
    spread = jax.random.uniform(key, (count,), jnp.float32, -0.5, 0.5)
    scale = ramp(count, 1.0)
    return scale * jnp.exp(spread)


def draw_norm_bias(key, part):
    key = jax.random.fold_in(key, 13)
    count = HEADS * HEAD_DIM
    base = 0.5 * jnp.clip(jax.random.normal(key, (count,), jnp.float32), -4.0, 4.0)
    scale = ramp(count, 1.0)
    return base * scale


def draw_first_moment(key, part):
    key = jax.random.fold_in(key, 14)
    count = HEADS * HEAD_DIM
    base = 30.0 * jnp.clip(jax.random.normal(key, (2, count), jnp.float32), -4.0, 4.0)
    scale = ramp(count, 1.0)
    return base * scale[None, :]


def draw_second_moment(key, part):
    key = jax.random.fold_in(key, 15)
    count = HEADS * HEAD_DIM
    level = jax.random.uniform(key, (2, count), jnp.float32, 9.2104, 11.5129)
    scale = ramp(count, 1.0)
    return jnp.exp(level) * scale[None, :]


def levels(rng, shape, shards, least, high):
    level, own = 1.0, jax.random.fold_in(rng, 6)
    for axis_at, shards_of in shards:
        heights = jnp.exp(jax.random.uniform(jax.random.fold_in(own, axis_at), (shards_of,), jnp.float32, least / len(shards), high / len(shards)))
        level = level * jnp.repeat(heights, shape[axis_at] // shards_of).reshape([-1 if axis == axis_at else 1 for axis in range(len(shape))])
    return level


def scatter_about(rng, shape, scale, most, cuts=(), kind=jnp.bfloat16):
    result = scale * jax.random.normal(rng, shape, jnp.float32)
    if cuts:
        result = result * levels(rng, shape, cuts, -0.22, 0.18)
    return jnp.clip(result, -most, most).astype(kind)


def setup_inputs(seed: int = 0) -> dict:
    splits = jax.random.split(jax.random.key(seed), 9)
    queries = scatter_about(splits[0], (TOKENS, CHANNELS), 1.0, 6.0, ((0, 128), (1, 4)))
    keys = scatter_about(splits[1], (TOKENS, CHANNELS), 1.0, 6.0, ((0, 128), (1, 4)))
    values = scatter_about(splits[2], (TOKENS, CHANNELS), 1.0, 6.0, ((0, 128), (1, 4)))
    grad_out = draw_grad_out(jax.random.fold_in(splits[8], 71), 0)
    norm_gain = draw_norm_gain(jax.random.fold_in(splits[8], 71), 0)
    norm_bias = draw_norm_bias(jax.random.fold_in(splits[8], 71), 0)
    first_moment = draw_first_moment(jax.random.fold_in(splits[8], 71), 0)
    second_moment = draw_second_moment(jax.random.fold_in(splits[8], 71), 0)
    return {"queries": queries, "keys": keys, "values": values, "grad_out": grad_out, "norm_gain": norm_gain, "norm_bias": norm_bias, "first_moment": first_moment, "second_moment": second_moment}


BETA_ONE = 0.9
BETA_TWO = 0.999
ADAM_EPS = 1e-06
DECAY_RATE = 0.01
LEARN_RATE = 0.2
NORM_EPS = 1e-05
TRUST_EPS = 1e-06
CORRECT_ONE = 1.0 - 0.9 ** 10
CORRECT_TWO = 1.0 - 0.999 ** 10

def rounded(array):
    return lax.optimization_barrier(array.astype(jnp.bfloat16)).astype(jnp.float32)

def group_norm_grads(output, grad_f, gain):
    center = output - lax.optimization_barrier(jnp.mean(output, axis=-1, keepdims=True))
    inv_std = lax.rsqrt(lax.optimization_barrier(jnp.mean(center * center, axis=-1, keepdims=True)) + NORM_EPS)
    normed = center * inv_std
    scaled = grad_f * gain
    d_out = inv_std * (scaled - lax.optimization_barrier(jnp.mean(scaled, axis=-1, keepdims=True)) - normed * lax.optimization_barrier(jnp.mean(scaled * normed, axis=-1, keepdims=True)))
    return (normed, d_out)

def lamb_direction(weight, grad, first, second):
    first_new = BETA_ONE * first + (1.0 - BETA_ONE) * grad
    second_new = BETA_TWO * second + (1.0 - BETA_TWO) * grad * grad
    return first_new / CORRECT_ONE / (jnp.sqrt(second_new / CORRECT_TWO) + ADAM_EPS) + DECAY_RATE * weight

def lamb_update(weight, grad, first, second):
    direction = lamb_direction(weight, grad, first, second)
    ratio = jnp.sqrt(jnp.sum(weight * weight)) / jnp.sqrt(jnp.sum(direction * direction) + TRUST_EPS)
    return weight - LEARN_RATE * ratio * direction

def reference(queries, keys, values, grad_out, norm_gain, norm_bias, first_moment, second_moment):
    blocks = TOKENS // SPAN

    def split(array):
        return array.reshape(blocks, SPAN, HEADS, HEAD_DIM)
    causal = jnp.arange(SPAN)[:, None] >= jnp.arange(SPAN)[None, :]

    def forward(state, pieces):
        query_c, key_c, value_c = [piece.astype(jnp.float32) for piece in pieces]
        scores = jnp.einsum('ihd,jhd->hij', query_c, key_c)
        weights = rounded(jnp.where(causal, scores, 0.0))
        state_r = rounded(state)
        output = jnp.einsum('hij,jhe->ihe', weights, value_c) + jnp.einsum('ihd,hde->ihe', query_c, state_r)
        return (state + jnp.einsum('jhd,jhe->hde', key_c, value_c), (output, state_r))
    empty_state = jnp.zeros((HEADS, HEAD_DIM, HEAD_DIM), jnp.float32)
    query_b, key_b, value_b = (split(queries), split(keys), split(values))
    final_state, (output, states) = lax.scan(forward, empty_state, (query_b, key_b, value_b))
    gain = norm_gain.reshape(HEADS, HEAD_DIM)
    grad_f = split(grad_out).astype(jnp.float32)
    normed, d_out = group_norm_grads(output, grad_f, gain)
    grad_gain = lax.optimization_barrier(jnp.sum(grad_f * normed, axis=(0, 1))).reshape(-1)
    grad_bias = lax.optimization_barrier(jnp.sum(grad_f, axis=(0, 1))).reshape(-1)
    dout_r = rounded(d_out)

    def backward(later, pieces):
        query_c, key_c, value_c = [piece.astype(jnp.float32) for piece in pieces[:3]]
        dout_c, state_r = (pieces[3], pieces[4])
        weights = rounded(jnp.where(causal, jnp.einsum('ihd,jhd->hij', query_c, key_c), 0.0))
        grad_w = rounded(jnp.where(causal, jnp.einsum('ihe,jhe->hij', dout_c, value_c), 0.0))
        later_r = rounded(later)
        grad_q = jnp.einsum('hij,jhd->ihd', grad_w, key_c) + jnp.einsum('ihe,hde->ihd', dout_c, state_r)
        grad_k = jnp.einsum('hij,ihd->jhd', grad_w, query_c) + jnp.einsum('jhe,hde->jhd', value_c, later_r)
        grad_v = jnp.einsum('hij,ihe->jhe', weights, dout_c) + jnp.einsum('jhd,hde->jhe', key_c, later_r)
        return (later + jnp.einsum('ihd,ihe->hde', query_c, dout_c), (grad_q, grad_k, grad_v))
    first_later, (grad_q, grad_k, grad_v) = lax.scan(backward, empty_state, (query_b, key_b, value_b, dout_r, states), reverse=True)
    shape_two = (TOKENS, HEADS * HEAD_DIM)
    new_gain = lamb_update(norm_gain, grad_gain, first_moment[0], second_moment[0])
    new_bias = lamb_update(norm_bias, grad_bias, first_moment[1], second_moment[1])
    return (grad_q.reshape(shape_two).astype(jnp.bfloat16), grad_k.reshape(shape_two).astype(jnp.bfloat16), grad_v.reshape(shape_two).astype(jnp.bfloat16), new_gain, new_bias)
```

```python
import functools

import jax
import jax.numpy as jnp
from jax import lax
from jax.experimental import pallas as pl
from jax.experimental.pallas import tpu as pltpu
from jax.sharding import Mesh
from jax.sharding import PartitionSpec as P

HEAD_DIM = 128
HEADS_HERE = 8
HALF = HEADS_HERE // 2
CORES = 2

BETA_ONE = 0.9
BETA_TWO = 0.999
ADAM_EPS = 1e-06
DECAY_RATE = 0.01
LEARN_RATE = 0.2
NORM_EPS = 1e-05
TRUST_EPS = 1e-06
CORRECT_ONE = 1.0 - 0.9**10
CORRECT_TWO = 1.0 - 0.999**10

F32 = jnp.float32
BF16 = jnp.bfloat16


def dot(a, b, da, db):
    return lax.dot_general(a, b, (((da,), (db,)), ((), ())), preferred_element_type=F32)


def cols(head):
    return pl.ds(pl.multiple_of(head * HEAD_DIM, HEAD_DIM), HEAD_DIM)


def causal_mask():
    row = lax.broadcasted_iota(jnp.int32, (HEAD_DIM, HEAD_DIM), 0)
    col = lax.broadcasted_iota(jnp.int32, (HEAD_DIM, HEAD_DIM), 1)
    return row >= col


def pair_kernel(core_ref, k_ref, v_ref, mine_ref, send_ref):
    core = core_ref[0]
    for out, half in ((send_ref, 1 - core), (mine_ref, core)):
        for j in range(HALF):
            at = cols(half * HALF + j)
            out[j] = dot(k_ref[:, at], v_ref[:, at], 0, 0)


def local_kernel(q_ref, k_ref, v_ref, w_ref, loc_ref):
    causal = causal_mask()
    for h in range(HEADS_HERE):
        at = slice(h * HEAD_DIM, (h + 1) * HEAD_DIM)
        scores = dot(q_ref[:, at], k_ref[:, at], 1, 1)
        w = jnp.where(causal, scores, 0.0).astype(BF16)
        w_ref[h] = w
        loc_ref[:, at] = dot(w, v_ref[:, at], 1, 0)


def scan_kernel(reverse, x_ref, o_ref):
    n = x_ref.shape[0]
    total = jnp.zeros(x_ref.shape[1:], F32)
    for i in reversed(range(n)) if reverse else range(n):
        o_ref[i] = total
        total = total + x_ref[i]


def norm_kernel(core_ref, q_ref, g_ref, gain_ref, loc_ref, own_ref, far_ref, state_ref, dout_ref, mine_ref, send_ref, grads_ref):
    core = core_ref[0]
    for half, source, out in ((core, own_ref, mine_ref), (1 - core, far_ref, send_ref)):
        for j in range(HALF):
            head = half * HALF + j
            at = cols(head)
            state = source[j].astype(BF16)
            state_ref[head] = state
            q = q_ref[:, at]
            output = loc_ref[:, at] + dot(q, state, 1, 0)
            center = output - jnp.mean(output, axis=-1, keepdims=True)
            inv_std = lax.rsqrt(jnp.mean(center * center, axis=-1, keepdims=True) + NORM_EPS)
            normed = center * inv_std
            grad_f = g_ref[:, at].astype(F32)
            scaled = grad_f * gain_ref[:, at]
            d_out = inv_std * (
                scaled
                - jnp.mean(scaled, axis=-1, keepdims=True)
                - normed * jnp.mean(scaled * normed, axis=-1, keepdims=True)
            )
            dout = d_out.astype(BF16)
            dout_ref[:, at] = dout
            out[j] = dot(q, dout, 0, 0)
            grads_ref[0:1, at] = jnp.sum(grad_f * normed, axis=0, keepdims=True)
            grads_ref[1:2, at] = jnp.sum(grad_f, axis=0, keepdims=True)


def near_kernel(q_ref, k_ref, v_ref, dout_ref, w_ref, state_ref, gq_ref, gk_ref, gv_ref):
    causal = causal_mask()
    for h in range(HEADS_HERE):
        at = slice(h * HEAD_DIM, (h + 1) * HEAD_DIM)
        dout = dout_ref[:, at]
        gw = jnp.where(causal, dot(dout, v_ref[:, at], 1, 1), 0.0).astype(BF16)
        gq_ref[:, at] = (dot(gw, k_ref[:, at], 1, 0) + dot(dout, state_ref[h], 1, 1)).astype(BF16)
        gk_ref[:, at] = dot(gw, q_ref[:, at], 0, 0)
        gv_ref[:, at] = dot(w_ref[h], dout, 0, 0)


def far_kernel(core_ref, k_ref, v_ref, gk_loc_ref, gv_loc_ref, own_ref, far_ref, gk_ref, gv_ref):
    core = core_ref[0]
    for half, source in ((core, own_ref), (1 - core, far_ref)):
        for j in range(HALF):
            at = cols(half * HALF + j)
            later = source[j].astype(BF16)
            gk_ref[:, at] = (gk_loc_ref[:, at] + dot(v_ref[:, at], later, 1, 1)).astype(BF16)
            gv_ref[:, at] = (gv_loc_ref[:, at] + dot(k_ref[:, at], later, 1, 0)).astype(BF16)


def call(kernel, outs, *args, scalar=False):
    vmem = pl.BlockSpec(memory_space=pltpu.VMEM)
    specs = [vmem] * len(args)
    if scalar:
        specs[0] = pl.BlockSpec(memory_space=pltpu.SMEM)
    return pl.pallas_call(
        kernel,
        out_shape=[jax.ShapeDtypeStruct(s, d) for s, d in outs],
        in_specs=specs,
        out_specs=[vmem] * len(outs),
        compiler_params=pltpu.CompilerParams(vmem_limit_bytes=32 * 1024 * 1024),
    )(*args)


def lamb_direction(weight, grad, first, second):
    first_new = BETA_ONE * first + (1.0 - BETA_ONE) * grad
    second_new = BETA_TWO * second + (1.0 - BETA_TWO) * grad * grad
    return (
        first_new / CORRECT_ONE / (jnp.sqrt(second_new / CORRECT_TWO) + ADAM_EPS)
        + DECAY_RATE * weight
    )


HALF_STATE = (HALF, HEAD_DIM, HEAD_DIM)


def swap(array):
    return lax.ppermute(array, "core", [(0, 1), (1, 0)])


def chip_scan(mine, arrived, reverse):
    chips = lax.axis_size("y") * lax.axis_size("z")
    pair = (mine + arrived).reshape(chips, -1, HEAD_DIM)
    landed = lax.all_to_all(pair, ("y", "z"), 0, 0, tiled=True)
    (sums,) = call(functools.partial(scan_kernel, reverse), [(landed.shape, F32)], landed)
    return lax.all_to_all(sums, ("y", "z"), 0, 0, tiled=True).reshape(HALF_STATE)


def per_device(queries, keys, values, grad_out, norm_gain, norm_bias, first_moment, second_moment):
    rows, width = queries.shape
    wide = (rows, width)
    states = (HEADS_HERE, HEAD_DIM, HEAD_DIM)
    core = lax.axis_index("core")
    core_s = core.astype(jnp.int32).reshape(1)

    mine, send = call(pair_kernel, [(HALF_STATE, F32)] * 2, core_s, keys, values, scalar=True)
    arrived = swap(send)
    weights, local = call(local_kernel, [(states, BF16), (wide, F32)], queries, keys, values)
    before = chip_scan(mine, arrived, False)
    far = swap(jnp.where(core == 0, before + mine, before))
    own = jnp.where(core == 1, before + arrived, before)

    state_b, dout, mine, send, grads = call(
        norm_kernel,
        [(states, BF16), (wide, BF16), (HALF_STATE, F32), (HALF_STATE, F32), ((2, width), F32)],
        core_s, queries, grad_out, norm_gain.reshape(1, width), local, own, far, scalar=True,
    )
    arrived = swap(send)
    grad_q, gk_loc, gv_loc = call(
        near_kernel, [(wide, BF16), (wide, F32), (wide, F32)], queries, keys, values, dout, weights, state_b
    )
    summed = lax.psum(lax.psum(lax.psum(grads, "core"), "z"), "y")
    after = chip_scan(mine, arrived, True)
    far = swap(jnp.where(core == 1, after + mine, after))
    own = jnp.where(core == 0, after + arrived, after)
    grad_k, grad_v = call(
        far_kernel, [(wide, BF16)] * 2, core_s, keys, values, gk_loc, gv_loc, own, far, scalar=True
    )

    weight = jnp.stack([norm_gain, norm_bias])
    step = lamb_direction(weight, summed, first_moment, second_moment)
    totals = jnp.stack([jnp.sum(weight * weight, axis=1), jnp.sum(step * step, axis=1)])
    totals = jnp.sum(lax.all_gather(totals, "fsdp"), axis=0)
    ratio = jnp.sqrt(totals[0]) / jnp.sqrt(totals[1] + TRUST_EPS)
    new = weight - LEARN_RATE * ratio[:, None] * step
    return grad_q, grad_k, grad_v, new[0], new[1]


def solution(mesh):
    seq, fsdp = mesh.devices.shape
    fine = Mesh(mesh.devices.reshape(4, seq // (4 * CORES), CORES, fsdp), ("y", "z", "core", "fsdp"))
    rows = ("y", "z", "core")
    big = P(rows, "fsdp")
    return jax.shard_map(
        per_device,
        mesh=fine,
        in_specs=(big, big, big, big, P("fsdp"), P("fsdp"), P(None, "fsdp"), P(None, "fsdp")),
        out_specs=(big, big, big, P("fsdp"), P("fsdp")),
        check_vma=False,
    )
```

```python
import functools

import jax
import jax.numpy as jnp
from jax import lax
from jax.experimental import pallas as pl
from jax.experimental.pallas import tpu as pltpu
from jax.sharding import Mesh
from jax.sharding import PartitionSpec as P

HEAD_DIM = 128
HEADS_HERE = 8
HALF = HEADS_HERE // 2
HALF_WIDTH = HALF * HEAD_DIM
CORES = 2
GROUP = 4
GRAD_ROWS = 8
VMEM_LIMIT = 12 * 1024 * 1024

BETA_ONE = 0.9
BETA_TWO = 0.999
ADAM_EPS = 1e-06
DECAY_RATE = 0.01
LEARN_RATE = 0.2
NORM_EPS = 1e-05
TRUST_EPS = 1e-06
CORRECT_ONE = 1.0 - 0.9**10
CORRECT_TWO = 1.0 - 0.999**10

F32 = jnp.float32
BF16 = jnp.bfloat16


def dot(a, b, da, db):
    return lax.dot_general(a, b, (((da,), (db,)), ((), ())), preferred_element_type=F32)


def cols(head):
    return pl.ds(pl.multiple_of(head * HEAD_DIM, HEAD_DIM), HEAD_DIM)


def causal_mask():
    row = lax.broadcasted_iota(jnp.int32, (HEAD_DIM, HEAD_DIM), 0)
    col = lax.broadcasted_iota(jnp.int32, (HEAD_DIM, HEAD_DIM), 1)
    return row >= col


def fixed(j):
    return slice(j * HEAD_DIM, (j + 1) * HEAD_DIM)


def pair_kernel(core_ref, k_hbm, v_hbm, mine_ref, send_ref, k_ref, v_ref, sems):
    copies = [
        pltpu.make_async_copy(src, dst, sems.at[i]) for i, (src, dst) in enumerate(((k_hbm, k_ref), (v_hbm, v_ref)))
    ]
    for copy in copies:
        copy.start()
    for copy in copies:
        copy.wait()
    core = core_ref[0]
    for out, half in ((send_ref, 1 - core), (mine_ref, core)):
        for j in range(HALF):
            at = cols(half * HALF + j)
            out[j] = dot(k_ref[:, at], v_ref[:, at], 0, 0)


def add_kernel(a_ref, b_ref, out_ref):
    rows = out_ref.shape[1]
    per = HEAD_DIM // rows
    for s in range(out_ref.shape[0]):
        at = slice((s % per) * rows, (s % per + 1) * rows)
        out_ref[s] = a_ref[s // per, at] + b_ref[s // per, at]


def widen_kernel(core_ref, q_ref, k_ref, v_ref, g_ref, send_ref):
    half = 1 - core_ref[0]
    at = pl.ds(pl.multiple_of(half * HALF_WIDTH, HALF_WIDTH), HALF_WIDTH)
    for i, ref in enumerate((q_ref, k_ref, v_ref, g_ref)):
        send_ref[i] = ref[:, at].astype(F32)


def local_kernel(core_ref, q_ref, k_ref, v_ref, recv_ref, w_ref, loc_ref):
    core = core_ref[0]
    causal = causal_mask()
    for j in range(HALF):
        at = cols(core * HALF + j)
        there = fixed(j)
        for b in range(CORES):
            if b == 0:
                q, k, v = q_ref[:, at], k_ref[:, at], v_ref[:, at]
            else:
                q, k, v = (recv_ref[i, :, there].astype(BF16) for i in range(3))
            w = jnp.where(causal, dot(q, k, 1, 1), 0.0).astype(BF16)
            w_ref[b, j] = w
            loc_ref[b, :, there] = dot(w, v, 1, 0)


def group_kernel(reverse, rows, h_ref, x_ref, part_ref, send_ref):
    h = h_ref[0]
    order = list(reversed(range(GROUP))) if reverse else list(range(GROUP))
    above = jnp.zeros((rows, HEAD_DIM), F32)
    for y in order:
        total = above
        for l in order:
            part_ref[y * GROUP + l] = total
            total = total + x_ref[y * GROUP + l, :rows]
        at = slice(y * rows, (y + 1) * rows)
        for i in range(GROUP):
            whole = (i < h) if reverse else (i > h)
            send_ref[i, at] = jnp.where(i == h, 0.0, jnp.where(whole, total, above))
        above = total
    if x_ref.shape[1] > rows:
        grads = x_ref[0, rows:]
        for i in range(1, x_ref.shape[0]):
            grads = grads + x_ref[i, rows:]
        for i in range(GROUP):
            send_ref[i, GROUP * rows :] = grads


def offset_kernel(rows, sent_ref, part_ref, out_ref, *grads_ref):
    for y in range(GROUP):
        at = slice(y * rows, (y + 1) * rows)
        offset = (sent_ref[0, at] + sent_ref[1, at]) + (sent_ref[2, at] + sent_ref[3, at])
        for l in range(GROUP):
            out_ref[y * GROUP + l] = part_ref[y * GROUP + l] + offset
    if grads_ref:
        at = slice(GROUP * rows, GROUP * rows + GRAD_ROWS)
        grads_ref[0][...] = (sent_ref[0, at] + sent_ref[1, at]) + (sent_ref[2, at] + sent_ref[3, at])


def norm_kernel(
    core_ref, q_ref, g_ref, gain_ref, recv_ref, loc_ref, before_ref, mine_ref, arrived_ref,
    state_ref, dout_ref, own_ref, other_ref, pay_ref,
):
    core = core_ref[0]
    slices, rows = pay_ref.shape[0] // HALF, pay_ref.shape[1] - GRAD_ROWS
    gain_rows, bias_rows = [], []
    for j in range(HALF):
        at = cols(core * HALF + j)
        there = fixed(j)
        gain = gain_ref[pl.ds(core * HALF + j, 1), :]
        before = before_ref[j]
        gain_row = jnp.zeros((1, HEAD_DIM), F32)
        bias_row = jnp.zeros((1, HEAD_DIM), F32)
        pair = None
        for b in range(CORES):
            if b == 0:
                q, grad_f = q_ref[:, at], g_ref[:, at].astype(F32)
                state = jnp.where(core == 1, before + arrived_ref[j], before).astype(BF16)
            else:
                q, grad_f = recv_ref[0, :, there].astype(BF16), recv_ref[3, :, there]
                state = jnp.where(core == 0, before + mine_ref[j], before).astype(BF16)
            state_ref[b, j] = state
            output = loc_ref[b, :, there] + dot(q, state, 1, 0)
            center = output - jnp.mean(output, axis=-1, keepdims=True)
            inv_std = lax.rsqrt(jnp.mean(center * center, axis=-1, keepdims=True) + NORM_EPS)
            normed = center * inv_std
            scaled = grad_f * gain
            d_out = inv_std * (
                scaled
                - jnp.mean(scaled, axis=-1, keepdims=True)
                - normed * jnp.mean(scaled * normed, axis=-1, keepdims=True)
            )
            dout = d_out.astype(BF16)
            dout_ref[b, :, there] = dout
            term = dot(q, dout, 0, 0)
            (own_ref, other_ref)[b][j] = term
            pair = term if pair is None else pair + term
            gain_row = gain_row + jnp.sum(grad_f * normed, axis=0, keepdims=True)
            bias_row = bias_row + jnp.sum(grad_f, axis=0, keepdims=True)
        for i in range(slices):
            pay_ref[j * slices + i, :rows] = pair[i * rows : (i + 1) * rows]
        gain_rows.append(gain_row)
        bias_rows.append(bias_row)
    grads = jnp.concatenate(gain_rows + bias_rows, axis=0)
    for s in range(pay_ref.shape[0]):
        pay_ref[s, rows:] = grads


def near_kernel(
    core_ref, q_ref, k_ref, v_ref, recv_ref, dout_ref, w_ref, state_ref, gq_ref, gk_ref, gv_ref, send_ref
):
    core = core_ref[0]
    causal = causal_mask()
    for j in range(HALF):
        at = cols(core * HALF + j)
        there = fixed(j)
        for b in range(CORES):
            if b == 0:
                q, k, v = q_ref[:, at], k_ref[:, at], v_ref[:, at]
            else:
                q, k, v = (recv_ref[i, :, there].astype(BF16) for i in range(3))
            dout = dout_ref[b, :, there]
            gw = jnp.where(causal, dot(dout, v, 1, 1), 0.0).astype(BF16)
            gq = dot(gw, k, 1, 0) + dot(dout, state_ref[b, j], 1, 1)
            gk = dot(gw, q, 0, 0)
            gv = dot(w_ref[b, j], dout, 0, 0)
            if b == 0:
                gq_ref[:, there], gk_ref[:, there], gv_ref[:, there] = gq.astype(BF16), gk, gv
            else:
                send_ref[0, :, there], send_ref[1, :, there], send_ref[2, :, there] = gq, gk, gv


def half_at(half):
    return pl.ds(pl.multiple_of(half * HALF_WIDTH, HALF_WIDTH), HALF_WIDTH)


def join_kernel(core_ref, own_ref, recv_ref, out_ref):
    core = core_ref[0]
    out_ref[:, half_at(core)] = own_ref[...]
    out_ref[:, half_at(1 - core)] = recv_ref[0].astype(BF16)


def far_kernel(
    core_ref, k_ref, v_ref, gk_own_ref, gv_own_ref, recv_ref, after_ref, other_ref, far_ref, gk_ref, gv_ref
):
    core = core_ref[0]
    for j in range(HALF):
        there = fixed(j)
        for b in range(CORES):
            if b == 0:
                at = cols(core * HALF + j)
                after = after_ref[j]
                later = jnp.where(core == 0, after + other_ref[j], after).astype(BF16)
                gk, gv = gk_own_ref[:, there], gv_own_ref[:, there]
            else:
                at = cols((1 - core) * HALF + j)
                later = far_ref[j].astype(BF16)
                gk, gv = recv_ref[1, :, there], recv_ref[2, :, there]
            gk_ref[:, at] = (gk + dot(v_ref[:, at], later, 1, 1)).astype(BF16)
            gv_ref[:, at] = (gv + dot(k_ref[:, at], later, 1, 0)).astype(BF16)


def lamb_direction(weight, grad, first, second):
    first_new = BETA_ONE * first + (1.0 - BETA_ONE) * grad
    second_new = BETA_TWO * second + (1.0 - BETA_TWO) * grad * grad
    return (
        first_new / CORRECT_ONE / (jnp.sqrt(second_new / CORRECT_TWO) + ADAM_EPS)
        + DECAY_RATE * weight
    )


def whole_sum(x):
    return jnp.sum(jnp.sum(x, axis=1, keepdims=True), axis=0, keepdims=True)


def step_kernel(core_ref, grads_ref, weight_ref, first_ref, second_ref, out_ref):
    at = pl.ds(core_ref[0] * HALF, HALF)
    for i in range(2):
        weight = weight_ref[i, at, :]
        step = lamb_direction(
            weight, grads_ref[i * HALF : (i + 1) * HALF], first_ref[i, at, :], second_ref[i, at, :]
        )
        out_ref[i * HALF : (i + 1) * HALF] = step
        for row, sum_of in ((8 + i, whole_sum(weight * weight)), (10 + i, whole_sum(step * step))):
            out_ref[row : row + 1] = jnp.broadcast_to(sum_of, (1, HEAD_DIM))
    out_ref[12:16] = jnp.zeros((4, HEAD_DIM), F32)


def new_kernel(core_ref, mine_ref, other_ref, sums_ref, weight_ref, out_ref):
    core = core_ref[0]
    for i in range(2):
        ratio = jnp.sqrt(sums_ref[i : i + 1]) / jnp.sqrt(sums_ref[2 + i : 3 + i] + TRUST_EPS)
        for half, ref in ((core, mine_ref), (1 - core, other_ref)):
            at = pl.ds(half * HALF, HALF)
            step = ref[i * HALF : (i + 1) * HALF]
            out_ref[i, at, :] = weight_ref[i, at, :] - LEARN_RATE * ratio * step


def call(kernel, outs, *args, scalar=True, hbm=False, scratch=()):
    vmem = pl.BlockSpec(memory_space=pltpu.VMEM)
    specs = [pl.BlockSpec(memory_space=pltpu.HBM) if hbm else vmem] * len(args)
    if scalar:
        specs[0] = pl.BlockSpec(memory_space=pltpu.SMEM)
    return pl.pallas_call(
        kernel,
        out_shape=[jax.ShapeDtypeStruct(s, d) for s, d in outs],
        in_specs=specs,
        out_specs=[vmem] * len(outs),
        scratch_shapes=scratch,
        compiler_params=pltpu.CompilerParams(vmem_limit_bytes=VMEM_LIMIT),
    )(*args)


STATE = (HALF, HEAD_DIM, HEAD_DIM)


def swap(array, axis="core", step=1):
    n = lax.axis_size(axis)
    return lax.ppermute(array, axis, [(i, i ^ step) for i in range(n)])


def exchange(array, axis):
    return lax.all_to_all(array, axis, 0, 0, tiled=True)


NEAR = ("y", "l")


def chip_scan(pay, reverse, beside):
    members = GROUP * GROUP
    rows = HALF * HEAD_DIM // members
    extra = pay.shape[1] - rows
    part = (members, rows, HEAD_DIM)
    h_s = lax.axis_index("h").astype(jnp.int32).reshape(1)
    landed = exchange(pay, NEAR)
    part_sums, send = call(
        functools.partial(group_kernel, reverse, rows),
        [(part, F32), ((GROUP, GROUP * rows + extra, HEAD_DIM), F32)], h_s, landed,
    )
    sent, beside = lax.optimization_barrier((exchange(send, "h"), beside))
    outs = [(part, F32)] + ([((extra, HEAD_DIM), F32)] if extra else [])
    sums, *rest = call(functools.partial(offset_kernel, rows), outs, sent, part_sums, scalar=False)
    return exchange(sums, NEAR).reshape(STATE), rest, beside


def per_device(queries, keys, values, grad_out, norm_gain, norm_bias, first_moment, second_moment):
    rows, width = queries.shape
    half = (rows, HALF_WIDTH)
    members = GROUP * GROUP
    slice_rows = HALF * HEAD_DIM // members
    core = lax.axis_index("core")
    core_s = core.astype(jnp.int32).reshape(1)
    by_head = (HEADS_HERE, HEAD_DIM)
    weight = jnp.stack([norm_gain.reshape(by_head), norm_bias.reshape(by_head)])
    first = first_moment.reshape((2,) + by_head)
    second = second_moment.reshape((2,) + by_head)

    mine, send = call(
        pair_kernel, [(STATE, F32)] * 2, core_s, keys, values, hbm=True,
        scratch=[pltpu.VMEM((rows, width), BF16)] * 2 + [pltpu.SemaphoreType.DMA((2,))],
    )
    arrived = swap(send)
    (pay,) = call(add_kernel, [((members, slice_rows, HEAD_DIM), F32)], mine, arrived, scalar=False)
    (wide,) = call(widen_kernel, [((4,) + half, F32)], core_s, queries, keys, values, grad_out)
    recv = swap(wide)
    weights, local = call(
        local_kernel, [((CORES,) + STATE, BF16), ((CORES,) + half, F32)], core_s, queries, keys, values, recv
    )
    before, _, (recv, weights, local) = chip_scan(pay, False, (recv, weights, local))

    pay_shape = (members, slice_rows + GRAD_ROWS, HEAD_DIM)
    state_b, dout, own, other, pay = call(
        norm_kernel,
        [((CORES,) + STATE, BF16), ((CORES,) + half, BF16), (STATE, F32), (STATE, F32), (pay_shape, F32)],
        core_s, queries, grad_out, weight[0], recv, local, before, mine, arrived,
    )
    gq_own, gk_own, gv_own, send = call(
        near_kernel,
        [(half, BF16), (half, F32), (half, F32), ((3,) + half, F32)],
        core_s, queries, keys, values, recv, dout, weights, state_b,
    )
    near = swap(send)
    (grad_q,) = call(join_kernel, [((rows, width), BF16)], core_s, gq_own, near)
    after, (grads,), (near, grad_q, gk_own, gv_own) = chip_scan(pay, True, (near, grad_q, gk_own, gv_own))

    (step,) = call(step_kernel, [((16, HEAD_DIM), F32)], core_s, grads, weight, first, second)
    step_there = swap(step)
    squares = step[8:] + step_there[8:]
    squares = lax.psum(squares, "fsdp")
    after, squares = lax.optimization_barrier((after, squares))
    (new,) = call(new_kernel, [((2,) + by_head, F32)], core_s, step, step_there, squares, weight)

    far = swap(jnp.where(core == 1, after + own, after))
    grad_k, grad_v = call(
        far_kernel, [((rows, width), BF16)] * 2,
        core_s, keys, values, gk_own, gv_own, near, after, other, far,
    )
    return grad_q, grad_k, grad_v, new[0].reshape(width), new[1].reshape(width)


def solution(mesh):
    seq, fsdp = mesh.devices.shape
    fine = Mesh(
        mesh.devices.reshape(GROUP, seq // (GROUP * GROUP * CORES), GROUP, CORES, fsdp), ("y", "h", "l", "core", "fsdp")
    )
    big = P(("y", "h", "l", "core"), "fsdp")
    return jax.shard_map(
        per_device,
        mesh=fine,
        in_specs=(big, big, big, big, P("fsdp"), P("fsdp"), P(None, "fsdp"), P(None, "fsdp")),
        out_specs=(big, big, big, P("fsdp"), P("fsdp")),
        check_vma=False,
    )
```

```python
import functools

import jax
import jax.numpy as jnp
from jax import lax
from jax.experimental import pallas as pl
from jax.experimental.pallas import tpu as pltpu
from jax.sharding import Mesh
from jax.sharding import PartitionSpec as P

HEAD_DIM = 128
HEADS_HERE = 8
HALF = HEADS_HERE // 2
HALF_WIDTH = HALF * HEAD_DIM
CORES = 2
GROUP = 4
GRAD_ROWS = 8
STEP_ROW = HALF * HEAD_DIM
VMEM_LIMIT = 12 * 1024 * 1024

BETA_ONE = 0.9
BETA_TWO = 0.999
ADAM_EPS = 1e-06
DECAY_RATE = 0.01
LEARN_RATE = 0.2
NORM_EPS = 1e-05
TRUST_EPS = 1e-06
CORRECT_ONE = 1.0 - 0.9**10
CORRECT_TWO = 1.0 - 0.999**10

F32 = jnp.float32
BF16 = jnp.bfloat16


def dot(a, b, da, db):
    return lax.dot_general(a, b, (((da,), (db,)), ((), ())), preferred_element_type=F32)


def cols(head):
    return pl.ds(pl.multiple_of(head * HEAD_DIM, HEAD_DIM), HEAD_DIM)


def causal_mask():
    row = lax.broadcasted_iota(jnp.int32, (HEAD_DIM, HEAD_DIM), 0)
    col = lax.broadcasted_iota(jnp.int32, (HEAD_DIM, HEAD_DIM), 1)
    return row >= col


def fixed(j):
    return slice(j * HEAD_DIM, (j + 1) * HEAD_DIM)


def pair_kernel(core_ref, kv_ref, mine_ref, send_ref):
    core = core_ref[0]
    k_ref, v_ref = kv_ref.at[0], kv_ref.at[1]
    for out, half in ((send_ref, 1 - core), (mine_ref, core)):
        for j in range(HALF):
            at = cols(half * HALF + j)
            out[j] = dot(k_ref[:, at], v_ref[:, at], 0, 0)


def add_kernel(core_ref, a_ref, b_ref, out_ref, first_ref):
    core = core_ref[0]
    for j in range(HALF):
        first_ref[j] = jnp.where(core == 0, a_ref[j], b_ref[j])
    rows = out_ref.shape[1]
    per = HEAD_DIM // rows
    for s in range(out_ref.shape[0]):
        at = slice((s % per) * rows, (s % per + 1) * rows)
        out_ref[s] = a_ref[s // per, at] + b_ref[s // per, at]


def widen_kernel(core_ref, q_ref, k_ref, v_ref, g_ref, send_ref):
    half = 1 - core_ref[0]
    at = pl.ds(pl.multiple_of(half * HALF_WIDTH, HALF_WIDTH), HALF_WIDTH)
    for i, ref in enumerate((q_ref, k_ref, v_ref, g_ref)):
        send_ref[i] = ref[:, at].astype(F32)


def local_kernel(core_ref, q_ref, k_ref, v_ref, g_ref, recv_ref, in_ref, loc_ref):
    core = core_ref[0]
    causal = causal_mask()
    at = half_at(core)
    for i, ref in enumerate((q_ref, k_ref, v_ref, g_ref)):
        in_ref[0, i] = ref[:, at]
        in_ref[1, i] = recv_ref[i].astype(BF16)
    for j in range(HALF):
        there = fixed(j)
        for b in range(CORES):
            q, k, v = (in_ref[b, i, :, there] for i in range(3))
            w = jnp.where(causal, dot(q, k, 1, 1), 0.0).astype(BF16)
            loc_ref[b, :, there] = dot(w, v, 1, 0)


def group_kernel(reverse, rows, x_ref, part_ref, send_ref):
    order = list(reversed(range(GROUP))) if reverse else list(range(GROUP))
    total = jnp.zeros((rows, HEAD_DIM), F32)
    for i, y in enumerate(order):
        for l in order:
            part_ref[y * GROUP + l] = total
            total = total + x_ref[y * GROUP + l, :rows]
        send_ref[i * rows : (i + 1) * rows] = total
    if x_ref.shape[1] > rows:
        grads = x_ref[0, rows:]
        for i in range(1, x_ref.shape[0]):
            grads = grads + x_ref[i, rows:]
        send_ref[GROUP * rows :] = grads


def sum_kernel(a_ref, b_ref, out_ref):
    out_ref[...] = a_ref[...] + b_ref[...]


def offset_kernel(reverse, rows, h_ref, near_ref, far_ref, mine_ref, part_ref, out_ref, *grads_ref):
    h = h_ref[0]
    order = list(reversed(range(GROUP))) if reverse else list(range(GROUP))
    near_first = ((h ^ 1) > h) if reverse else ((h ^ 1) < h)
    far_first = ((h ^ 3) > h) if reverse else ((h ^ 3) < h)
    zero = jnp.zeros((rows, HEAD_DIM), F32)
    for i, y in enumerate(order):
        offset = zero
        for ref, first in ((near_ref, near_first), (far_ref, far_first)):
            up_to = ref[i * rows : (i + 1) * rows]
            above = ref[(i - 1) * rows : i * rows] if i else zero
            offset = offset + jnp.where(first, up_to, above)
        for l in range(GROUP):
            out_ref[y * GROUP + l] = part_ref[y * GROUP + l] + offset
    if grads_ref:
        grads_ref[0][...] = mine_ref[GROUP * rows :] + far_ref[GROUP * rows :]


def norm_kernel(core_ref, in_ref, gain_ref, loc_ref, before_ref, first_ref, state_ref, dout_ref, pay_ref):
    core = core_ref[0]
    slices, rows = pay_ref.shape[0] // HALF, pay_ref.shape[1] - GRAD_ROWS
    gain_rows, bias_rows = [], []
    for j in range(HALF):
        there = fixed(j)
        gain = gain_ref[pl.ds(core * HALF + j, 1), :]
        before = before_ref[j]
        pair, gain_row, bias_row = 0.0, 0.0, 0.0
        for b in range(CORES):
            state = jnp.where(core != b, before + first_ref[j], before).astype(BF16)
            state_ref[b, j] = state
            q, grad_f = in_ref[b, 0, :, there], in_ref[b, 3, :, there].astype(F32)
            output = loc_ref[b, :, there] + dot(q, state, 1, 0)
            center = output - jnp.mean(output, axis=-1, keepdims=True)
            inv_std = lax.rsqrt(jnp.mean(center * center, axis=-1, keepdims=True) + NORM_EPS)
            normed = center * inv_std
            scaled = grad_f * gain
            d_out = inv_std * (
                scaled
                - jnp.mean(scaled, axis=-1, keepdims=True)
                - normed * jnp.mean(scaled * normed, axis=-1, keepdims=True)
            )
            dout = d_out.astype(BF16)
            dout_ref[b, :, there] = dout
            pair = pair + dot(q, dout, 0, 0)
            gain_row = gain_row + jnp.sum(grad_f * normed, axis=0, keepdims=True)
            bias_row = bias_row + jnp.sum(grad_f, axis=0, keepdims=True)
        for i in range(slices):
            pay_ref[j * slices + i, :rows] = pair[i * rows : (i + 1) * rows]
        gain_rows.append(gain_row)
        bias_rows.append(bias_row)
    grads = jnp.concatenate(gain_rows + bias_rows, axis=0)
    for s in range(pay_ref.shape[0]):
        pay_ref[s, rows:] = grads


def near_kernel(
    core_ref, in_ref, dout_ref, state_ref, gain_ref, bias_ref, first_ref, second_ref,
    gq_ref, gk_ref, gv_ref, send_ref, own_ref, other_ref, pack_ref,
):
    core = core_ref[0]
    for p, ref in enumerate((gain_ref, bias_ref)):
        pack_ref[0, p * HALF : (p + 1) * HALF] = ref[pl.ds(core * HALF, HALF), :]
        for j in range(HALF):
            at, row = cols(core * HALF + j), p * HALF + j
            pack_ref[1, row : row + 1] = first_ref[p : p + 1, at]
            pack_ref[2, row : row + 1] = second_ref[p : p + 1, at]
    causal = causal_mask()
    for j in range(HALF):
        there = fixed(j)
        for b in range(CORES):
            q, k, v = (in_ref[b, i, :, there] for i in range(3))
            dout = dout_ref[b, :, there]
            (own_ref, other_ref)[b][j] = dot(q, dout, 0, 0)
            w = jnp.where(causal, dot(q, k, 1, 1), 0.0).astype(BF16)
            gw = jnp.where(causal, dot(dout, v, 1, 1), 0.0).astype(BF16)
            gq = dot(gw, k, 1, 0) + dot(dout, state_ref[b, j], 1, 1)
            gk = dot(gw, q, 0, 0)
            gv = dot(w, dout, 0, 0)
            if b == 0:
                gq_ref[:, there], gk_ref[:, there], gv_ref[:, there] = gq.astype(BF16), gk, gv
            else:
                send_ref[0, :, there], send_ref[1, :, there], send_ref[2, :, there] = gq, gk, gv


def half_at(half):
    return pl.ds(pl.multiple_of(half * HALF_WIDTH, HALF_WIDTH), HALF_WIDTH)


def join_kernel(core_ref, own_ref, recv_ref, out_ref):
    core = core_ref[0]
    out_ref[:, half_at(core)] = own_ref[...]
    out_ref[:, half_at(1 - core)] = recv_ref[0].astype(BF16)


def lamb_direction(weight, grad, first, second):
    first_new = BETA_ONE * first + (1.0 - BETA_ONE) * grad
    second_new = BETA_TWO * second + (1.0 - BETA_TWO) * grad * grad
    return (
        first_new / CORRECT_ONE / (jnp.sqrt(second_new / CORRECT_TWO) + ADAM_EPS)
        + DECAY_RATE * weight
    )


def whole_sum(x):
    return jnp.sum(jnp.sum(x, axis=1, keepdims=True), axis=0, keepdims=True)


def step_kernel(grads_ref, pack_ref, step_ref, squares_ref):
    for i in range(2):
        at = slice(i * HALF, (i + 1) * HALF)
        weight = pack_ref[0, at]
        step = lamb_direction(weight, grads_ref[at], pack_ref[1, at], pack_ref[2, at])
        step_ref[at] = step
        for row, sum_of in ((i, whole_sum(weight * weight)), (2 + i, whole_sum(step * step))):
            squares_ref[row : row + 1] = jnp.broadcast_to(sum_of, (1, HEAD_DIM))
    squares_ref[4:8] = jnp.zeros((4, HEAD_DIM), F32)


def pack_kernel(core_ref, after_ref, own_ref, step_ref, squares_ref, out_ref):
    core = core_ref[0]
    for j in range(HALF):
        after = after_ref[j]
        out_ref[j * HEAD_DIM : (j + 1) * HEAD_DIM] = jnp.where(core == 1, after + own_ref[j], after)
    out_ref[STEP_ROW : STEP_ROW + 8] = step_ref[...]
    out_ref[STEP_ROW + 8 :] = squares_ref[...]


def far_kernel(
    core_ref, k_ref, v_ref, gk_own_ref, gv_own_ref, recv_ref, after_ref, other_ref, far_ref, step_ref, squares_ref,
    gain_ref, bias_ref, gk_ref, gv_ref, new_gain_ref, new_bias_ref,
):
    core = core_ref[0]
    for j in range(HALF):
        there = fixed(j)
        for b in range(CORES):
            if b == 0:
                at = cols(core * HALF + j)
                after = after_ref[j]
                later = jnp.where(core == 0, after + other_ref[j], after).astype(BF16)
                gk, gv = gk_own_ref[:, there], gv_own_ref[:, there]
            else:
                at = cols((1 - core) * HALF + j)
                later = far_ref[there].astype(BF16)
                gk, gv = recv_ref[1, :, there], recv_ref[2, :, there]
            gk_ref[:, at] = (gk + dot(v_ref[:, at], later, 1, 1)).astype(BF16)
            gv_ref[:, at] = (gv + dot(k_ref[:, at], later, 1, 0)).astype(BF16)
    squares = squares_ref[...] + far_ref[STEP_ROW + 8 :]
    for i, (weight_ref, out) in enumerate(((gain_ref, new_gain_ref), (bias_ref, new_bias_ref))):
        ratio = jnp.sqrt(squares[i : i + 1]) / jnp.sqrt(squares[2 + i : 3 + i] + TRUST_EPS)
        steps = (step_ref[i * HALF : (i + 1) * HALF], far_ref[STEP_ROW + i * HALF : STEP_ROW + (i + 1) * HALF])
        for half, step in zip((core, 1 - core), steps):
            at = pl.ds(half * HALF, HALF)
            out[at, :] = weight_ref[at, :] - LEARN_RATE * ratio * step


def call(kernel, outs, *args, scalar=True):
    vmem = pl.BlockSpec(memory_space=pltpu.VMEM)
    specs = [vmem] * len(args)
    if scalar:
        specs[0] = pl.BlockSpec(memory_space=pltpu.SMEM)
    return pl.pallas_call(
        kernel,
        out_shape=[jax.ShapeDtypeStruct(s, d) for s, d in outs],
        in_specs=specs,
        out_specs=[vmem] * len(outs),
        compiler_params=pltpu.CompilerParams(vmem_limit_bytes=VMEM_LIMIT),
    )(*args)


STATE = (HALF, HEAD_DIM, HEAD_DIM)


def swap(array, axis="core", step=1):
    n = lax.axis_size(axis)
    return lax.ppermute(array, axis, [(i, i ^ step) for i in range(n)])


def exchange(array, axis):
    return lax.all_to_all(array, axis, 0, 0, tiled=True)


NEAR = ("y", "l")


def chip_scan(pay, reverse, beside_one, beside_two, given):
    members = GROUP * GROUP
    rows = HALF * HEAD_DIM // members
    extra = pay.shape[1] - rows
    part = (members, rows, HEAD_DIM)
    h_s = lax.axis_index("h").astype(jnp.int32).reshape(1)
    landed = exchange(pay, NEAR)
    if reverse:
        landed, given = lax.optimization_barrier((landed, given))
    sums_shape = (GROUP * rows + extra, HEAD_DIM)
    part_sums, send = call(
        functools.partial(group_kernel, reverse, rows), [(part, F32), (sums_shape, F32)], landed, scalar=False
    )
    near, given = lax.optimization_barrier((swap(send, "h", 1), beside_one(given)))
    (both,) = call(sum_kernel, [(sums_shape, F32)], send, near, scalar=False)
    far, made = lax.optimization_barrier((swap(both, "h", 3), beside_two(given)))
    outs = [(part, F32)] + ([((extra, HEAD_DIM), F32)] if extra else [])
    sums, *rest = call(functools.partial(offset_kernel, reverse, rows), outs, h_s, near, far, both, part_sums)
    return exchange(sums, NEAR).reshape(STATE), rest, made


def per_device(queries, keys, values, grad_out, norm_gain, norm_bias, first_moment, second_moment):
    rows, width = queries.shape
    half = (rows, HALF_WIDTH)
    members = GROUP * GROUP
    slice_rows = HALF * HEAD_DIM // members
    core_s = lax.axis_index("core").astype(jnp.int32).reshape(1)
    by_head = (HEADS_HERE, HEAD_DIM)
    gain, bias = norm_gain.reshape(by_head), norm_bias.reshape(by_head)

    def share_inputs():
        (wide,) = call(widen_kernel, [((4,) + half, F32)], core_s, queries, keys, values, grad_out)
        return swap(wide)

    def local_part(recv):
        return call(
            local_kernel, [((CORES, 4) + half, BF16), ((CORES,) + half, F32)],
            core_s, queries, keys, values, grad_out, recv,
        )

    def near_grads(both, dout, state):
        return call(
            near_kernel,
            [(half, BF16), (half, F32), (half, F32), ((3,) + half, F32), (STATE, F32), (STATE, F32), ((3,) + by_head, F32)],
            core_s, both, dout, state, gain, bias, first_moment, second_moment,
        )

    def share_grads(gq_own, gk_own, gv_own, send, own, other, pack):
        near = swap(send)
        (grad_q,) = call(join_kernel, [((rows, width), BF16)], core_s, gq_own, near)
        return grad_q, gk_own, gv_own, near, own, other, pack

    mine, send = call(pair_kernel, [(STATE, F32)] * 2, core_s, jnp.stack([keys, values]))
    pay, first_state = call(
        add_kernel, [((members, slice_rows, HEAD_DIM), F32), (STATE, F32)], core_s, mine, swap(send)
    )
    before, _, (both, local) = chip_scan(pay, False, lambda recv: recv, local_part, share_inputs())

    pay_shape = (members, slice_rows + GRAD_ROWS, HEAD_DIM)
    state, dout, pay = call(
        norm_kernel,
        [((CORES,) + STATE, BF16), ((CORES,) + half, BF16), (pay_shape, F32)],
        core_s, both, gain, local, before, first_state,
    )
    after, (grads,), (grad_q, gk_own, gv_own, near, own, other, pack) = chip_scan(
        pay, True, lambda tied: near_grads(*tied), lambda tied: share_grads(*tied), (both, dout, state)
    )

    step, squares = call(step_kernel, [(by_head, F32)] * 2, grads, pack, scalar=False)
    after, squares = lax.optimization_barrier((after, lax.psum(squares, "fsdp")))
    (send,) = call(pack_kernel, [((STEP_ROW + 16, HEAD_DIM), F32)], core_s, after, own, step, squares)
    far = swap(send)
    grad_k, grad_v, new_gain, new_bias = call(
        far_kernel, [((rows, width), BF16)] * 2 + [(by_head, F32)] * 2,
        core_s, keys, values, gk_own, gv_own, near, after, other, far, step, squares, gain, bias,
    )
    return grad_q, grad_k, grad_v, new_gain.reshape(width), new_bias.reshape(width)


def solution(mesh):
    seq, fsdp = mesh.devices.shape
    fine = Mesh(
        mesh.devices.reshape(GROUP, seq // (GROUP * GROUP * CORES), GROUP, CORES, fsdp), ("y", "h", "l", "core", "fsdp")
    )
    big = P(("y", "h", "l", "core"), "fsdp")
    return jax.shard_map(
        per_device,
        mesh=fine,
        in_specs=(big, big, big, big, P("fsdp"), P("fsdp"), P(None, "fsdp"), P(None, "fsdp")),
        out_specs=(big, big, big, P("fsdp"), P("fsdp")),
        check_vma=False,
    )
```

```python
import functools

import jax
import jax.numpy as jnp
from jax import lax
from jax.experimental import pallas as pl
from jax.experimental.pallas import tpu as pltpu
from jax.sharding import Mesh
from jax.sharding import PartitionSpec as P

HEAD_DIM = 128
HEADS_HERE = 8
HALF = HEADS_HERE // 2
HALF_WIDTH = HALF * HEAD_DIM
CORES = 2
GROUP = 4
GRAD_ROWS = 8
STEP_ROW = HALF * HEAD_DIM
VMEM_LIMIT = 12 * 1024 * 1024

BETA_ONE = 0.9
BETA_TWO = 0.999
ADAM_EPS = 1e-06
DECAY_RATE = 0.01
LEARN_RATE = 0.2
NORM_EPS = 1e-05
TRUST_EPS = 1e-06
CORRECT_ONE = 1.0 - 0.9**10
CORRECT_TWO = 1.0 - 0.999**10

F32 = jnp.float32
BF16 = jnp.bfloat16


def dot(a, b, da, db):
    return lax.dot_general(a, b, (((da,), (db,)), ((), ())), preferred_element_type=F32)


def cols(head):
    return pl.ds(pl.multiple_of(head * HEAD_DIM, HEAD_DIM), HEAD_DIM)


def causal_mask():
    row = lax.broadcasted_iota(jnp.int32, (HEAD_DIM, HEAD_DIM), 0)
    col = lax.broadcasted_iota(jnp.int32, (HEAD_DIM, HEAD_DIM), 1)
    return row >= col


def fixed(j):
    return slice(j * HEAD_DIM, (j + 1) * HEAD_DIM)


def pair_kernel(core_ref, kv_ref, mine_ref, send_ref):
    core = core_ref[0]
    k_ref, v_ref = kv_ref.at[0], kv_ref.at[1]
    for out, half in ((send_ref, 1 - core), (mine_ref, core)):
        for j in range(HALF):
            at = cols(half * HALF + j)
            out[j] = dot(k_ref[:, at], v_ref[:, at], 0, 0)


def add_kernel(a_ref, b_ref, out_ref):
    rows = out_ref.shape[1]
    per = HEAD_DIM // rows
    for s in range(out_ref.shape[0]):
        at = slice((s % per) * rows, (s % per + 1) * rows)
        out_ref[s] = a_ref[s // per, at] + b_ref[s // per, at]


def widen_kernel(core_ref, q_ref, k_ref, v_ref, g_ref, send_ref):
    half = 1 - core_ref[0]
    at = pl.ds(pl.multiple_of(half * HALF_WIDTH, HALF_WIDTH), HALF_WIDTH)
    for i, ref in enumerate((q_ref, k_ref, v_ref, g_ref)):
        send_ref[i] = ref[:, at].astype(F32)


def local_kernel(core_ref, q_ref, k_ref, v_ref, g_ref, recv_ref, in_ref, loc_ref, first_ref):
    core = core_ref[0]
    causal = causal_mask()
    at = half_at(core)
    for i, ref in enumerate((q_ref, k_ref, v_ref, g_ref)):
        in_ref[0, i] = ref[:, at]
        in_ref[1, i] = recv_ref[i].astype(BF16)
    for j in range(HALF):
        there = fixed(j)
        first_ref[j] = dot(in_ref[core, 1, :, there], in_ref[core, 2, :, there], 0, 0)
        for b in range(CORES):
            q, k, v = (in_ref[b, i, :, there] for i in range(3))
            w = jnp.where(causal, dot(q, k, 1, 1), 0.0).astype(BF16)
            loc_ref[b, :, there] = dot(w, v, 1, 0)


def group_kernel(reverse, rows, x_ref, part_ref, send_ref):
    order = list(reversed(range(GROUP))) if reverse else list(range(GROUP))
    total = jnp.zeros((rows, HEAD_DIM), F32)
    for i, y in enumerate(order):
        for l in order:
            part_ref[y * GROUP + l] = total
            total = total + x_ref[y * GROUP + l, :rows]
        send_ref[i * rows : (i + 1) * rows] = total
    if x_ref.shape[1] > rows:
        grads = x_ref[0, rows:]
        for i in range(1, x_ref.shape[0]):
            grads = grads + x_ref[i, rows:]
        send_ref[GROUP * rows :] = grads


def for_group(reverse, rows, ref, i, group, dest):
    first = (group > dest) if reverse else (group < dest)
    up_to = ref[i * rows : (i + 1) * rows]
    above = ref[(i - 1) * rows : i * rows] if i else jnp.zeros((rows, HEAD_DIM), F32)
    return jnp.where(first, up_to, above)


def partners(at_ref):
    h, core = at_ref[0] // CORES, at_ref[0] % CORES
    return h, h ^ (1 + 2 * core), h ^ (3 - 2 * core)


def sum_kernel(reverse, rows, at_ref, mine_ref, near_ref, out_ref):
    h, near, far = partners(at_ref)
    for i in range(GROUP):
        own = for_group(reverse, rows, mine_ref, i, h, far)
        out_ref[i * rows : (i + 1) * rows] = own + for_group(reverse, rows, near_ref, i, near, far)
    if out_ref.shape[0] > GROUP * rows:
        out_ref[GROUP * rows :] = mine_ref[GROUP * rows :] + near_ref[GROUP * rows :]


def offset_kernel(reverse, rows, at_ref, near_ref, far_ref, mine_ref, part_ref, out_ref, *grads_ref):
    h, near, _ = partners(at_ref)
    for i, y in enumerate(reversed(range(GROUP)) if reverse else range(GROUP)):
        offset = for_group(reverse, rows, near_ref, i, near, h) + far_ref[i * rows : (i + 1) * rows]
        for l in range(GROUP):
            out_ref[y * GROUP + l] = part_ref[y * GROUP + l] + offset
    if grads_ref:
        grads_ref[0][...] = mine_ref[GROUP * rows :] + far_ref[GROUP * rows :]


def norm_kernel(core_ref, in_ref, gain_ref, loc_ref, before_ref, first_ref, state_ref, dout_ref, pay_ref):
    core = core_ref[0]
    slices, rows = pay_ref.shape[0] // HALF, pay_ref.shape[1] - GRAD_ROWS
    gain_rows, bias_rows = [], []
    for j in range(HALF):
        there = fixed(j)
        gain = gain_ref[pl.ds(core * HALF + j, 1), :]
        before = before_ref[j]
        pair, gain_row, bias_row = 0.0, 0.0, 0.0
        for b in range(CORES):
            state = jnp.where(core != b, before + first_ref[j], before).astype(BF16)
            state_ref[b, j] = state
            q, grad_f = in_ref[b, 0, :, there], in_ref[b, 3, :, there].astype(F32)
            output = loc_ref[b, :, there] + dot(q, state, 1, 0)
            center = output - jnp.mean(output, axis=-1, keepdims=True)
            inv_std = lax.rsqrt(jnp.mean(center * center, axis=-1, keepdims=True) + NORM_EPS)
            normed = center * inv_std
            scaled = grad_f * gain
            d_out = inv_std * (
                scaled
                - jnp.mean(scaled, axis=-1, keepdims=True)
                - normed * jnp.mean(scaled * normed, axis=-1, keepdims=True)
            )
            dout = d_out.astype(BF16)
            dout_ref[b, :, there] = dout
            pair = pair + dot(q, dout, 0, 0)
            gain_row = gain_row + jnp.sum(grad_f * normed, axis=0, keepdims=True)
            bias_row = bias_row + jnp.sum(grad_f, axis=0, keepdims=True)
        for i in range(slices):
            pay_ref[j * slices + i, :rows] = pair[i * rows : (i + 1) * rows]
        gain_rows.append(gain_row)
        bias_rows.append(bias_row)
    grads = jnp.concatenate(gain_rows + bias_rows, axis=0)
    for s in range(pay_ref.shape[0]):
        pay_ref[s, rows:] = grads


def near_kernel(
    core_ref, in_ref, dout_ref, state_ref, gain_ref, bias_ref, first_ref, second_ref,
    gq_ref, gk_ref, gv_ref, send_ref, own_ref, other_ref, pack_ref,
):
    core = core_ref[0]
    for p, ref in enumerate((gain_ref, bias_ref)):
        pack_ref[0, p * HALF : (p + 1) * HALF] = ref[pl.ds(core * HALF, HALF), :]
        for j in range(HALF):
            at, row = cols(core * HALF + j), p * HALF + j
            pack_ref[1, row : row + 1] = first_ref[p : p + 1, at]
            pack_ref[2, row : row + 1] = second_ref[p : p + 1, at]
    causal = causal_mask()
    for j in range(HALF):
        there = fixed(j)
        for b in range(CORES):
            q, k, v = (in_ref[b, i, :, there] for i in range(3))
            dout = dout_ref[b, :, there]
            (own_ref, other_ref)[b][j] = dot(q, dout, 0, 0)
            w = jnp.where(causal, dot(q, k, 1, 1), 0.0).astype(BF16)
            gw = jnp.where(causal, dot(dout, v, 1, 1), 0.0).astype(BF16)
            gq = dot(gw, k, 1, 0) + dot(dout, state_ref[b, j], 1, 1)
            gk = dot(gw, q, 0, 0)
            gv = dot(w, dout, 0, 0)
            if b == 0:
                gq_ref[:, there], gk_ref[:, there], gv_ref[:, there] = gq.astype(BF16), gk, gv
            else:
                send_ref[0, :, there], send_ref[1, :, there], send_ref[2, :, there] = gq, gk, gv


def half_at(half):
    return pl.ds(pl.multiple_of(half * HALF_WIDTH, HALF_WIDTH), HALF_WIDTH)


def join_kernel(core_ref, own_ref, recv_ref, out_ref):
    core = core_ref[0]
    out_ref[:, half_at(core)] = own_ref[...]
    out_ref[:, half_at(1 - core)] = recv_ref[0].astype(BF16)


def lamb_direction(weight, grad, first, second):
    first_new = BETA_ONE * first + (1.0 - BETA_ONE) * grad
    second_new = BETA_TWO * second + (1.0 - BETA_TWO) * grad * grad
    return (
        first_new / CORRECT_ONE / (jnp.sqrt(second_new / CORRECT_TWO) + ADAM_EPS)
        + DECAY_RATE * weight
    )


def whole_sum(x):
    return jnp.sum(jnp.sum(x, axis=1, keepdims=True), axis=0, keepdims=True)


def step_kernel(grads_ref, pack_ref, step_ref, squares_ref):
    for i in range(2):
        at = slice(i * HALF, (i + 1) * HALF)
        weight = pack_ref[0, at]
        step = lamb_direction(weight, grads_ref[at], pack_ref[1, at], pack_ref[2, at])
        step_ref[at] = step
        for row, sum_of in ((i, whole_sum(weight * weight)), (2 + i, whole_sum(step * step))):
            squares_ref[row : row + 1] = jnp.broadcast_to(sum_of, (1, HEAD_DIM))
    squares_ref[4:8] = jnp.zeros((4, HEAD_DIM), F32)


def pack_kernel(core_ref, after_ref, own_ref, step_ref, squares_ref, out_ref):
    core = core_ref[0]
    for j in range(HALF):
        after = after_ref[j]
        out_ref[j * HEAD_DIM : (j + 1) * HEAD_DIM] = jnp.where(core == 1, after + own_ref[j], after)
    out_ref[STEP_ROW : STEP_ROW + 8] = step_ref[...]
    out_ref[STEP_ROW + 8 :] = squares_ref[...]


def far_kernel(
    core_ref, k_ref, v_ref, gk_own_ref, gv_own_ref, recv_ref, after_ref, other_ref, far_ref, step_ref, squares_ref,
    gain_ref, bias_ref, gk_ref, gv_ref, new_gain_ref, new_bias_ref,
):
    core = core_ref[0]
    for j in range(HALF):
        there = fixed(j)
        for b in range(CORES):
            if b == 0:
                at = cols(core * HALF + j)
                after = after_ref[j]
                later = jnp.where(core == 0, after + other_ref[j], after).astype(BF16)
                gk, gv = gk_own_ref[:, there], gv_own_ref[:, there]
            else:
                at = cols((1 - core) * HALF + j)
                later = far_ref[there].astype(BF16)
                gk, gv = recv_ref[1, :, there], recv_ref[2, :, there]
            gk_ref[:, at] = (gk + dot(v_ref[:, at], later, 1, 1)).astype(BF16)
            gv_ref[:, at] = (gv + dot(k_ref[:, at], later, 1, 0)).astype(BF16)
    squares = squares_ref[...] + far_ref[STEP_ROW + 8 :]
    for i, (weight_ref, out) in enumerate(((gain_ref, new_gain_ref), (bias_ref, new_bias_ref))):
        ratio = jnp.sqrt(squares[i : i + 1]) / jnp.sqrt(squares[2 + i : 3 + i] + TRUST_EPS)
        steps = (step_ref[i * HALF : (i + 1) * HALF], far_ref[STEP_ROW + i * HALF : STEP_ROW + (i + 1) * HALF])
        for half, step in zip((core, 1 - core), steps):
            at = pl.ds(half * HALF, HALF)
            out[at, :] = weight_ref[at, :] - LEARN_RATE * ratio * step


def call(kernel, outs, *args, scalar=True):
    vmem = pl.BlockSpec(memory_space=pltpu.VMEM)
    specs = [vmem] * len(args)
    if scalar:
        specs[0] = pl.BlockSpec(memory_space=pltpu.SMEM)
    return pl.pallas_call(
        kernel,
        out_shape=[jax.ShapeDtypeStruct(s, d) for s, d in outs],
        in_specs=specs,
        out_specs=[vmem] * len(outs),
        compiler_params=pltpu.CompilerParams(vmem_limit_bytes=VMEM_LIMIT),
    )(*args)


STATE = (HALF, HEAD_DIM, HEAD_DIM)


def swap(array, axis="core", step=1):
    n = lax.axis_size(axis)
    return lax.ppermute(array, axis, [(i, i ^ step) for i in range(n)])


def group_swap(array, steps):
    pairs = [(h * CORES + c, (h ^ steps[c]) * CORES + c) for h in range(GROUP) for c in range(CORES)]
    return lax.ppermute(array, ("h", "core"), pairs)


def exchange(array, axis):
    return lax.all_to_all(array, axis, 0, 0, tiled=True)


NEAR = ("y", "l")


def chip_scan(pay, reverse, beside_one, beside_two, given):
    members = GROUP * GROUP
    rows = HALF * HEAD_DIM // members
    extra = pay.shape[1] - rows
    part = (members, rows, HEAD_DIM)
    at_s = lax.axis_index(("h", "core")).astype(jnp.int32).reshape(1)
    landed = exchange(pay, NEAR)
    if reverse:
        landed, given = lax.optimization_barrier((landed, given))
    sums_shape = (GROUP * rows + extra, HEAD_DIM)
    part_sums, send = call(
        functools.partial(group_kernel, reverse, rows), [(part, F32), (sums_shape, F32)], landed, scalar=False
    )
    near, given = lax.optimization_barrier((group_swap(send, (1, 3)), beside_one(given)))
    (both,) = call(functools.partial(sum_kernel, reverse, rows), [(sums_shape, F32)], at_s, send, near)
    far, made = lax.optimization_barrier((group_swap(both, (3, 1)), beside_two(given)))
    outs = [(part, F32)] + ([((extra, HEAD_DIM), F32)] if extra else [])
    sums, *rest = call(functools.partial(offset_kernel, reverse, rows), outs, at_s, near, far, both, part_sums)
    return exchange(sums, NEAR).reshape(STATE), rest, made


def per_device(queries, keys, values, grad_out, norm_gain, norm_bias, first_moment, second_moment):
    rows, width = queries.shape
    half = (rows, HALF_WIDTH)
    members = GROUP * GROUP
    slice_rows = HALF * HEAD_DIM // members
    core_s = lax.axis_index("core").astype(jnp.int32).reshape(1)
    by_head = (HEADS_HERE, HEAD_DIM)
    gain, bias = norm_gain.reshape(by_head), norm_bias.reshape(by_head)

    def share_inputs():
        (wide,) = call(widen_kernel, [((4,) + half, F32)], core_s, queries, keys, values, grad_out)
        return swap(wide)

    def local_part(recv):
        return call(
            local_kernel, [((CORES, 4) + half, BF16), ((CORES,) + half, F32), (STATE, F32)],
            core_s, queries, keys, values, grad_out, recv,
        )

    def near_grads(both, dout, state):
        return call(
            near_kernel,
            [(half, BF16), (half, F32), (half, F32), ((3,) + half, F32), (STATE, F32), (STATE, F32), ((3,) + by_head, F32)],
            core_s, both, dout, state, gain, bias, first_moment, second_moment,
        )

    def share_grads(gq_own, gk_own, gv_own, send, own, other, pack):
        near = swap(send)
        (grad_q,) = call(join_kernel, [((rows, width), BF16)], core_s, gq_own, near)
        return grad_q, gk_own, gv_own, near, own, other, pack

    mine, send = call(pair_kernel, [(STATE, F32)] * 2, core_s, jnp.stack([keys, values]))
    (pay,) = call(add_kernel, [((members, slice_rows, HEAD_DIM), F32)], mine, swap(send), scalar=False)
    before, _, (both, local, first_state) = chip_scan(pay, False, lambda recv: recv, local_part, share_inputs())

    pay_shape = (members, slice_rows + GRAD_ROWS, HEAD_DIM)
    state, dout, pay = call(
        norm_kernel,
        [((CORES,) + STATE, BF16), ((CORES,) + half, BF16), (pay_shape, F32)],
        core_s, both, gain, local, before, first_state,
    )
    after, (grads,), (grad_q, gk_own, gv_own, near, own, other, pack) = chip_scan(
        pay, True, lambda tied: near_grads(*tied), lambda tied: share_grads(*tied), (both, dout, state)
    )

    step, squares = call(step_kernel, [(by_head, F32)] * 2, grads, pack, scalar=False)
    after, squares = lax.optimization_barrier((after, lax.psum(squares, "fsdp")))
    (send,) = call(pack_kernel, [((STEP_ROW + 16, HEAD_DIM), F32)], core_s, after, own, step, squares)
    far = swap(send)
    grad_k, grad_v, new_gain, new_bias = call(
        far_kernel, [((rows, width), BF16)] * 2 + [(by_head, F32)] * 2,
        core_s, keys, values, gk_own, gv_own, near, after, other, far, step, squares, gain, bias,
    )
    return grad_q, grad_k, grad_v, new_gain.reshape(width), new_bias.reshape(width)


def solution(mesh):
    seq, fsdp = mesh.devices.shape
    fine = Mesh(
        mesh.devices.reshape(GROUP, seq // (GROUP * GROUP * CORES), GROUP, CORES, fsdp), ("y", "h", "l", "core", "fsdp")
    )
    big = P(("y", "h", "l", "core"), "fsdp")
    return jax.shard_map(
        per_device,
        mesh=fine,
        in_specs=(big, big, big, big, P("fsdp"), P("fsdp"), P(None, "fsdp"), P(None, "fsdp")),
        out_specs=(big, big, big, P("fsdp"), P("fsdp")),
        check_vma=False,
    )
```

```python
import functools

import jax
import jax.numpy as jnp
from jax import lax
from jax.experimental import pallas as pl
from jax.experimental.pallas import tpu as pltpu
from jax.sharding import PartitionSpec as P

HEAD_DIM = 128
HEADS_HERE = 8
HALF = HEADS_HERE // 2
HALF_WIDTH = HALF * HEAD_DIM
CORES = 2
GROUP = 4
GRAD_ROWS = 8
ORDER = [(0, 0), (0, 1), (0, 2), (0, 3), (1, 0), (1, 1), (1, 2), (1, 3), (2, 0), (2, 1), (2, 2), (2, 3), (3, 0), (3, 1), (3, 2), (3, 3)]
SLOT = [[0, 1, 2, 3], [4, 5, 6, 7], [8, 9, 10, 11], [12, 13, 14, 15]]
STEP_ROW = HALF * HEAD_DIM
VMEM_LIMIT = 12 * 1024 * 1024

BETA_ONE = 0.9
BETA_TWO = 0.999
ADAM_EPS = 1e-06
DECAY_RATE = 0.01
LEARN_RATE = 0.2
NORM_EPS = 1e-05
TRUST_EPS = 1e-06
CORRECT_ONE = 1.0 - 0.9**10
CORRECT_TWO = 1.0 - 0.999**10

F32 = jnp.float32
BF16 = jnp.bfloat16


def dot(a, b, da, db):
    return lax.dot_general(a, b, (((da,), (db,)), ((), ())), preferred_element_type=F32)


def cols(head):
    return pl.ds(pl.multiple_of(head * HEAD_DIM, HEAD_DIM), HEAD_DIM)


def causal_mask():
    row = lax.broadcasted_iota(jnp.int32, (HEAD_DIM, HEAD_DIM), 0)
    col = lax.broadcasted_iota(jnp.int32, (HEAD_DIM, HEAD_DIM), 1)
    return row >= col


def fixed(j):
    return slice(j * HEAD_DIM, (j + 1) * HEAD_DIM)


def pair_kernel(core_ref, kv_ref, mine_ref, send_ref):
    core = core_ref[0]
    k_ref, v_ref = kv_ref.at[0], kv_ref.at[1]
    for out, half in ((send_ref, 1 - core), (mine_ref, core)):
        for j in range(HALF):
            at = cols(half * HALF + j)
            out[j] = dot(k_ref[:, at], v_ref[:, at], 0, 0)


def add_kernel(a_ref, b_ref, out_ref):
    rows = out_ref.shape[1]
    per = HEAD_DIM // rows
    for s in range(out_ref.shape[0]):
        at = slice((s % per) * rows, (s % per + 1) * rows)
        out_ref[s] = a_ref[s // per, at] + b_ref[s // per, at]


def widen_kernel(core_ref, q_ref, k_ref, v_ref, g_ref, send_ref):
    half = 1 - core_ref[0]
    at = pl.ds(pl.multiple_of(half * HALF_WIDTH, HALF_WIDTH), HALF_WIDTH)
    for i, ref in enumerate((q_ref, k_ref, v_ref, g_ref)):
        send_ref[i] = ref[:, at].astype(F32)


def local_kernel(core_ref, q_ref, k_ref, v_ref, g_ref, recv_ref, in_ref, loc_ref, first_ref):
    core = core_ref[0]
    causal = causal_mask()
    at = half_at(core)
    for i, ref in enumerate((q_ref, k_ref, v_ref, g_ref)):
        in_ref[0, i] = ref[:, at]
        in_ref[1, i] = recv_ref[i].astype(BF16)
    for j in range(HALF):
        there = fixed(j)
        first_ref[j] = dot(in_ref[core, 1, :, there], in_ref[core, 2, :, there], 0, 0)
        for b in range(CORES):
            q, k, v = (in_ref[b, i, :, there] for i in range(3))
            w = jnp.where(causal, dot(q, k, 1, 1), 0.0).astype(BF16)
            loc_ref[b, :, there] = dot(w, v, 1, 0)


def place(at_ref):
    h, core = at_ref[0] // CORES, at_ref[0] % CORES
    return core, h, h ^ (1 + 2 * core), h ^ (3 - 2 * core)


def is_split(core, group):
    return core == 2


def orders(reverse):
    order = list(reversed(range(GROUP))) if reverse else list(range(GROUP))
    return order, order[2:] + order[:2]


def group_kernel(reverse, rows, at_ref, x_ref, part_ref, send_ref):
    core, h, _, _ = place(at_ref)
    split = is_split(core, h)
    order, turned = orders(reverse)
    above = jnp.zeros((rows, HEAD_DIM), F32)
    for i, y in enumerate(order):
        x = [x_ref[SLOT[y][l], :rows] for l in range(GROUP)]
        part, total = {}, above
        for l in order:
            part[l] = total
            total = total + x[l]
        half = above
        for k, l in enumerate(turned):
            part_ref[SLOT[y][l]] = jnp.where(split, half, part[l])
            half = half + x[l]
            if k == 1:
                send_ref[i * rows : (i + 1) * rows] = jnp.where(split, half, total)
        above = total
    if x_ref.shape[1] > rows:
        grads = x_ref[0, rows:]
        for i in range(1, x_ref.shape[0]):
            grads = grads + x_ref[i, rows:]
        send_ref[GROUP * rows :] = grads


def up_to(rows, ref, i):
    return ref[i * rows : (i + 1) * rows] if i >= 0 else jnp.zeros((rows, HEAD_DIM), F32)


def for_group(reverse, rows, ref, i, core, group, dest):
    first = (group > dest) if reverse else (group < dest)
    with_this = jnp.logical_or(first, is_split(core, group))
    return jnp.where(with_this, up_to(rows, ref, i), up_to(rows, ref, i - 1))


def sum_kernel(reverse, rows, at_ref, mine_ref, near_ref, out_ref):
    core, h, near, far = place(at_ref)
    to_split = is_split(core, far)
    for i in range(GROUP):
        plain = up_to(rows, mine_ref, i) + up_to(rows, near_ref, i)
        made = for_group(reverse, rows, mine_ref, i, core, h, far)
        made = made + for_group(reverse, rows, near_ref, i, core, near, far)
        out_ref[i * rows : (i + 1) * rows] = jnp.where(to_split, plain, made)
    if out_ref.shape[0] > GROUP * rows:
        out_ref[GROUP * rows :] = mine_ref[GROUP * rows :] + near_ref[GROUP * rows :]


def offset_kernel(reverse, rows, at_ref, near_ref, far_ref, mine_ref, part_ref, out_ref, *grads_ref):
    core, h, near, _ = place(at_ref)
    split = is_split(core, h)
    order, turned = orders(reverse)
    for i, y in enumerate(order):
        offset = for_group(reverse, rows, near_ref, i, core, near, h) + up_to(rows, far_ref, i)
        halves = [up_to(rows, near_ref, n) + up_to(rows, far_ref, n) for n in (i - 1, i)]
        halves = [jnp.where(split, half, offset) for half in halves]
        for k, l in enumerate(turned):
            out_ref[SLOT[y][l]] = part_ref[SLOT[y][l]] + halves[k // 2]
    if grads_ref:
        grads_ref[0][...] = mine_ref[GROUP * rows :] + far_ref[GROUP * rows :]


def norm_kernel(core_ref, in_ref, gain_ref, loc_ref, before_ref, first_ref, state_ref, dout_ref, pay_ref):
    core = core_ref[0]
    slices, rows = pay_ref.shape[0] // HALF, pay_ref.shape[1] - GRAD_ROWS
    gain_rows, bias_rows = [], []
    for j in range(HALF):
        there = fixed(j)
        gain = gain_ref[pl.ds(core * HALF + j, 1), :]
        before = before_ref[j]
        pair, gain_row, bias_row = 0.0, 0.0, 0.0
        for b in range(CORES):
            state = jnp.where(core != b, before + first_ref[j], before).astype(BF16)
            state_ref[b, j] = state
            q, grad_f = in_ref[b, 0, :, there], in_ref[b, 3, :, there].astype(F32)
            output = loc_ref[b, :, there] + dot(q, state, 1, 0)
            center = output - jnp.mean(output, axis=-1, keepdims=True)
            inv_std = lax.rsqrt(jnp.mean(center * center, axis=-1, keepdims=True) + NORM_EPS)
            normed = center * inv_std
            scaled = grad_f * gain
            d_out = inv_std * (
                scaled
                - jnp.mean(scaled, axis=-1, keepdims=True)
                - normed * jnp.mean(scaled * normed, axis=-1, keepdims=True)
            )
            dout = d_out.astype(BF16)
            dout_ref[b, :, there] = dout
            pair = pair + dot(q, dout, 0, 0)
            gain_row = gain_row + jnp.sum(grad_f * normed, axis=0, keepdims=True)
            bias_row = bias_row + jnp.sum(grad_f, axis=0, keepdims=True)
        for i in range(slices):
            pay_ref[j * slices + i, :rows] = pair[i * rows : (i + 1) * rows]
        gain_rows.append(gain_row)
        bias_rows.append(bias_row)
    grads = jnp.concatenate(gain_rows + bias_rows, axis=0)
    for s in range(pay_ref.shape[0]):
        pay_ref[s, rows:] = grads


def near_kernel(
    core_ref, in_ref, dout_ref, state_ref, gain_ref, bias_ref, first_ref, second_ref,
    gq_ref, gk_ref, gv_ref, send_ref, own_ref, other_ref, pack_ref,
):
    core = core_ref[0]
    for p, ref in enumerate((gain_ref, bias_ref)):
        pack_ref[0, p * HALF : (p + 1) * HALF] = ref[pl.ds(core * HALF, HALF), :]
        for j in range(HALF):
            at, row = cols(core * HALF + j), p * HALF + j
            pack_ref[1, row : row + 1] = first_ref[p : p + 1, at]
            pack_ref[2, row : row + 1] = second_ref[p : p + 1, at]
    causal = causal_mask()
    for j in range(HALF):
        there = fixed(j)
        for b in range(CORES):
            q, k, v = (in_ref[b, i, :, there] for i in range(3))
            dout = dout_ref[b, :, there]
            (own_ref, other_ref)[b][j] = dot(q, dout, 0, 0)
            w = jnp.where(causal, dot(q, k, 1, 1), 0.0).astype(BF16)
            gw = jnp.where(causal, dot(dout, v, 1, 1), 0.0).astype(BF16)
            gq = dot(gw, k, 1, 0) + dot(dout, state_ref[b, j], 1, 1)
            gk = dot(gw, q, 0, 0)
            gv = dot(w, dout, 0, 0)
            if b == 0:
                gq_ref[:, there], gk_ref[:, there], gv_ref[:, there] = gq.astype(BF16), gk, gv
            else:
                send_ref[0, :, there], send_ref[1, :, there], send_ref[2, :, there] = gq, gk, gv


def half_at(half):
    return pl.ds(pl.multiple_of(half * HALF_WIDTH, HALF_WIDTH), HALF_WIDTH)


def join_kernel(core_ref, own_ref, recv_ref, out_ref):
    core = core_ref[0]
    out_ref[:, half_at(core)] = own_ref[...]
    out_ref[:, half_at(1 - core)] = recv_ref[0].astype(BF16)


def lamb_direction(weight, grad, first, second):
    first_new = BETA_ONE * first + (1.0 - BETA_ONE) * grad
    second_new = BETA_TWO * second + (1.0 - BETA_TWO) * grad * grad
    return (
        first_new / CORRECT_ONE / (jnp.sqrt(second_new / CORRECT_TWO) + ADAM_EPS)
        + DECAY_RATE * weight
    )


def whole_sum(x):
    return jnp.sum(jnp.sum(x, axis=1, keepdims=True), axis=0, keepdims=True)


def step_kernel(grads_ref, pack_ref, step_ref, squares_ref):
    for i in range(2):
        at = slice(i * HALF, (i + 1) * HALF)
        weight = pack_ref[0, at]
        step = lamb_direction(weight, grads_ref[at], pack_ref[1, at], pack_ref[2, at])
        step_ref[at] = step
        for row, sum_of in ((i, whole_sum(weight * weight)), (2 + i, whole_sum(step * step))):
            squares_ref[row : row + 1] = jnp.broadcast_to(sum_of, (1, HEAD_DIM))
    squares_ref[4:8] = jnp.zeros((4, HEAD_DIM), F32)


def pack_kernel(core_ref, after_ref, own_ref, step_ref, squares_ref, out_ref):
    core = core_ref[0]
    for j in range(HALF):
        after = after_ref[j]
        out_ref[j * HEAD_DIM : (j + 1) * HEAD_DIM] = jnp.where(core == 1, after + own_ref[j], after)
    out_ref[STEP_ROW : STEP_ROW + 8] = step_ref[...]
    out_ref[STEP_ROW + 8 :] = squares_ref[...]


def far_kernel(
    core_ref, k_ref, v_ref, gk_own_ref, gv_own_ref, recv_ref, after_ref, other_ref, far_ref, step_ref, squares_ref,
    gain_ref, bias_ref, gk_ref, gv_ref, new_gain_ref, new_bias_ref,
):
    core = core_ref[0]
    for j in range(HALF):
        there = fixed(j)
        for b in range(CORES):
            if b == 0:
                at = cols(core * HALF + j)
                after = after_ref[j]
                later = jnp.where(core == 0, after + other_ref[j], after).astype(BF16)
                gk, gv = gk_own_ref[:, there], gv_own_ref[:, there]
            else:
                at = cols((1 - core) * HALF + j)
                later = far_ref[there].astype(BF16)
                gk, gv = recv_ref[1, :, there], recv_ref[2, :, there]
            gk_ref[:, at] = (gk + dot(v_ref[:, at], later, 1, 1)).astype(BF16)
            gv_ref[:, at] = (gv + dot(k_ref[:, at], later, 1, 0)).astype(BF16)
    squares = squares_ref[...] + far_ref[STEP_ROW + 8 :]
    for i, (weight_ref, out) in enumerate(((gain_ref, new_gain_ref), (bias_ref, new_bias_ref))):
        ratio = jnp.sqrt(squares[i : i + 1]) / jnp.sqrt(squares[2 + i : 3 + i] + TRUST_EPS)
        steps = (step_ref[i * HALF : (i + 1) * HALF], far_ref[STEP_ROW + i * HALF : STEP_ROW + (i + 1) * HALF])
        for half, step in zip((core, 1 - core), steps):
            at = pl.ds(half * HALF, HALF)
            out[at, :] = weight_ref[at, :] - LEARN_RATE * ratio * step


def call(kernel, outs, *args, scalar=True):
    vmem = pl.BlockSpec(memory_space=pltpu.VMEM)
    specs = [vmem] * len(args)
    if scalar:
        specs[0] = pl.BlockSpec(memory_space=pltpu.SMEM)
    return pl.pallas_call(
        kernel,
        out_shape=[jax.ShapeDtypeStruct(s, d) for s, d in outs],
        in_specs=specs,
        out_specs=[vmem] * len(outs),
        compiler_params=pltpu.CompilerParams(vmem_limit_bytes=VMEM_LIMIT),
    )(*args)


STATE = (HALF, HEAD_DIM, HEAD_DIM)


def swap(array, axis="seq"):
    n = lax.axis_size(axis)
    return lax.ppermute(array, axis, [(i, i ^ 1) for i in range(n)])


def device(ring, y, h, l, core):
    return (y * ring + (h * GROUP + l) % ring) * CORES + core


def group_swap(array, steps):
    ring = lax.axis_size("seq") // (GROUP * CORES)
    pairs = [
        (device(ring, y, h, l, core), device(ring, y, h ^ steps[core], l, core))
        for y in range(GROUP) for h in range(GROUP) for l in range(GROUP) for core in range(CORES)
    ]
    return lax.ppermute(array, "seq", pairs)


def exchange(array):
    ring = lax.axis_size("seq") // (GROUP * CORES)
    groups = [
        [device(ring, y, h, l, core) for y, l in ORDER]
        for h in range(GROUP) for core in range(CORES)
    ]
    return lax.all_to_all(array, "seq", 0, 0, tiled=True, axis_index_groups=groups)


def chip_scan(pay, reverse, beside_one, beside_two, given):
    members = GROUP * GROUP
    rows = HALF * HEAD_DIM // members
    extra = pay.shape[1] - rows
    part = (members, rows, HEAD_DIM)
    at = lax.axis_index("seq").astype(jnp.int32)
    ring = lax.axis_size("seq") // (GROUP * CORES)
    core = at % CORES
    at_s = ((at // CORES + ring) % ring // GROUP * CORES + core).reshape(1)
    landed = exchange(pay)
    if reverse:
        landed, given = lax.optimization_barrier((landed, given))
    sums_shape = (GROUP * rows + extra, HEAD_DIM)
    part_sums, send = call(
        functools.partial(group_kernel, reverse, rows), [(part, F32), (sums_shape, F32)], at_s, landed
    )
    near, given = lax.optimization_barrier((group_swap(send, (1, 3)), beside_one(given)))
    (both,) = call(functools.partial(sum_kernel, reverse, rows), [(sums_shape, F32)], at_s, send, near)
    far, made = lax.optimization_barrier((group_swap(both, (3, 1)), beside_two(given)))
    outs = [(part, F32)] + ([((extra, HEAD_DIM), F32)] if extra else [])
    sums, *rest = call(functools.partial(offset_kernel, reverse, rows), outs, at_s, near, far, both, part_sums)
    return exchange(sums).reshape(STATE), rest, made


def per_device(queries, keys, values, grad_out, norm_gain, norm_bias, first_moment, second_moment):
    rows, width = queries.shape
    half = (rows, HALF_WIDTH)
    members = GROUP * GROUP
    slice_rows = HALF * HEAD_DIM // members
    core_s = (lax.axis_index("seq").astype(jnp.int32) % CORES).reshape(1)
    by_head = (HEADS_HERE, HEAD_DIM)
    gain, bias = norm_gain.reshape(by_head), norm_bias.reshape(by_head)

    def share_inputs():
        (wide,) = call(widen_kernel, [((4,) + half, F32)], core_s, queries, keys, values, grad_out)
        return swap(wide)

    def local_part(recv):
        return call(
            local_kernel, [((CORES, 4) + half, BF16), ((CORES,) + half, F32), (STATE, F32)],
            core_s, queries, keys, values, grad_out, recv,
        )

    def near_grads(both, dout, state):
        return call(
            near_kernel,
            [(half, BF16), (half, F32), (half, F32), ((3,) + half, F32), (STATE, F32), (STATE, F32), ((3,) + by_head, F32)],
            core_s, both, dout, state, gain, bias, first_moment, second_moment,
        )

    def share_grads(gq_own, gk_own, gv_own, send, own, other, pack):
        near = swap(send)
        (grad_q,) = call(join_kernel, [((rows, width), BF16)], core_s, gq_own, near)
        return grad_q, gk_own, gv_own, near, own, other, pack

    mine, send = call(pair_kernel, [(STATE, F32)] * 2, core_s, jnp.stack([keys, values]))
    (pay,) = call(add_kernel, [((members, slice_rows, HEAD_DIM), F32)], mine, swap(send), scalar=False)
    before, _, (both, local, first_state) = chip_scan(pay, False, lambda recv: recv, local_part, share_inputs())

    pay_shape = (members, slice_rows + GRAD_ROWS, HEAD_DIM)
    state, dout, pay = call(
        norm_kernel,
        [((CORES,) + STATE, BF16), ((CORES,) + half, BF16), (pay_shape, F32)],
        core_s, both, gain, local, before, first_state,
    )
    after, (grads,), (grad_q, gk_own, gv_own, near, own, other, pack) = chip_scan(
        pay, True, lambda tied: near_grads(*tied), lambda tied: share_grads(*tied), (both, dout, state)
    )

    step, squares = call(step_kernel, [(by_head, F32)] * 2, grads, pack, scalar=False)
    after, squares = lax.optimization_barrier((after, lax.psum(squares, "fsdp")))
    (send,) = call(pack_kernel, [((STEP_ROW + 16, HEAD_DIM), F32)], core_s, after, own, step, squares)
    far = swap(send)
    grad_k, grad_v, new_gain, new_bias = call(
        far_kernel, [((rows, width), BF16)] * 2 + [(by_head, F32)] * 2,
        core_s, keys, values, gk_own, gv_own, near, after, other, far, step, squares, gain, bias,
    )
    return grad_q, grad_k, grad_v, new_gain.reshape(width), new_bias.reshape(width)


def solution(mesh):
    big = P("seq", "fsdp")
    return jax.shard_map(
        per_device,
        mesh=mesh,
        in_specs=(big, big, big, big, P("fsdp"), P("fsdp"), P(None, "fsdp"), P(None, "fsdp")),
        out_specs=(big, big, big, P("fsdp"), P("fsdp")),
        check_vma=False,
    )
```

```python
import functools

import jax
import jax.numpy as jnp
from jax import lax
from jax.experimental import pallas as pl
from jax.experimental.pallas import tpu as pltpu
from jax.sharding import Mesh
from jax.sharding import PartitionSpec as P

HEAD_DIM = 128
HEADS_HERE = 8
HALF = HEADS_HERE // 2
HALF_WIDTH = HALF * HEAD_DIM
CORES = 2
GROUP = 4
GRAD_ROWS = 8
STEP_ROW = HALF * HEAD_DIM
VMEM_LIMIT = 12 * 1024 * 1024

BETA_ONE = 0.9
BETA_TWO = 0.999
ADAM_EPS = 1e-06
DECAY_RATE = 0.01
LEARN_RATE = 0.2
NORM_EPS = 1e-05
TRUST_EPS = 1e-06
CORRECT_ONE = 1.0 - 0.9**10
CORRECT_TWO = 1.0 - 0.999**10

F32 = jnp.float32
BF16 = jnp.bfloat16


def dot(a, b, da, db):
    return lax.dot_general(a, b, (((da,), (db,)), ((), ())), preferred_element_type=F32)


def cols(head):
    return pl.ds(pl.multiple_of(head * HEAD_DIM, HEAD_DIM), HEAD_DIM)


def causal_mask():
    row = lax.broadcasted_iota(jnp.int32, (HEAD_DIM, HEAD_DIM), 0)
    col = lax.broadcasted_iota(jnp.int32, (HEAD_DIM, HEAD_DIM), 1)
    return row >= col


def fixed(j):
    return slice(j * HEAD_DIM, (j + 1) * HEAD_DIM)


def pair_kernel(core_ref, kv_ref, mine_ref, send_ref):
    core = core_ref[0]
    k_ref, v_ref = kv_ref.at[0], kv_ref.at[1]
    for out, half in ((send_ref, 1 - core), (mine_ref, core)):
        for j in range(HALF):
            at = cols(half * HALF + j)
            out[j] = dot(k_ref[:, at], v_ref[:, at], 0, 0)


def add_kernel(a_ref, b_ref, out_ref):
    rows = out_ref.shape[1]
    per = HEAD_DIM // rows
    for s in range(out_ref.shape[0]):
        at = slice((s % per) * rows, (s % per + 1) * rows)
        out_ref[s] = a_ref[s // per, at] + b_ref[s // per, at]


def widen_kernel(core_ref, q_ref, k_ref, v_ref, g_ref, send_ref):
    half = 1 - core_ref[0]
    at = pl.ds(pl.multiple_of(half * HALF_WIDTH, HALF_WIDTH), HALF_WIDTH)
    for i, ref in enumerate((q_ref, k_ref, v_ref, g_ref)):
        send_ref[i] = ref[:, at].astype(F32)


def local_kernel(core_ref, q_ref, k_ref, v_ref, g_ref, recv_ref, in_ref, loc_ref, first_ref, bias_ref):
    core = core_ref[0]
    causal = causal_mask()
    at = half_at(core)
    for i, ref in enumerate((q_ref, k_ref, v_ref, g_ref)):
        in_ref[0, i] = ref[:, at]
        in_ref[1, i] = recv_ref[i].astype(BF16)
    for j in range(HALF):
        there = fixed(j)
        first_ref[j] = dot(in_ref[core, 1, :, there], in_ref[core, 2, :, there], 0, 0)
        grad_f = in_ref[0, 3, :, there].astype(F32) + in_ref[1, 3, :, there].astype(F32)
        bias_ref[j : j + 1] = jnp.sum(grad_f, axis=0, keepdims=True)
        for b in range(CORES):
            q, k, v = (in_ref[b, i, :, there] for i in range(3))
            w = jnp.where(causal, dot(q, k, 1, 1), 0.0).astype(BF16)
            loc_ref[b, :, there] = dot(w, v, 1, 0)


def group_kernel(reverse, rows, x_ref, part_ref, send_ref):
    order = list(reversed(range(GROUP))) if reverse else list(range(GROUP))
    total = jnp.zeros((rows, HEAD_DIM), F32)
    for i, y in enumerate(order):
        for l in order:
            part_ref[y * GROUP + l] = total
            total = total + x_ref[y * GROUP + l, :rows]
        send_ref[i * rows : (i + 1) * rows] = total
    if x_ref.shape[1] > rows:
        grads = x_ref[0, rows:]
        for i in range(1, x_ref.shape[0]):
            grads = grads + x_ref[i, rows:]
        send_ref[GROUP * rows :] = grads


def for_group(reverse, rows, ref, i, group, dest):
    first = (group > dest) if reverse else (group < dest)
    up_to = ref[i * rows : (i + 1) * rows]
    above = ref[(i - 1) * rows : i * rows] if i else jnp.zeros((rows, HEAD_DIM), F32)
    return jnp.where(first, up_to, above)


def partners(at_ref):
    h, core = at_ref[0] // CORES, at_ref[0] % CORES
    return h, h ^ (1 + 2 * core), h ^ (3 - 2 * core)


def sum_kernel(reverse, rows, at_ref, mine_ref, near_ref, out_ref):
    h, near, far = partners(at_ref)
    for i in range(GROUP):
        own = for_group(reverse, rows, mine_ref, i, h, far)
        out_ref[i * rows : (i + 1) * rows] = own + for_group(reverse, rows, near_ref, i, near, far)
    if out_ref.shape[0] > GROUP * rows:
        out_ref[GROUP * rows :] = mine_ref[GROUP * rows :] + near_ref[GROUP * rows :]


def offset_kernel(reverse, rows, at_ref, near_ref, far_ref, mine_ref, part_ref, out_ref, *grads_ref):
    h, near, _ = partners(at_ref)
    for i, y in enumerate(reversed(range(GROUP)) if reverse else range(GROUP)):
        offset = for_group(reverse, rows, near_ref, i, near, h) + far_ref[i * rows : (i + 1) * rows]
        for l in range(GROUP):
            out_ref[y * GROUP + l] = part_ref[y * GROUP + l] + offset
    if grads_ref:
        grads_ref[0][...] = mine_ref[GROUP * rows :] + far_ref[GROUP * rows :]


def norm_kernel(core_ref, in_ref, gain_ref, loc_ref, before_ref, first_ref, bias_ref, state_ref, dout_ref, pay_ref):
    core = core_ref[0]
    slices, rows = pay_ref.shape[0] // HALF, pay_ref.shape[1] - GRAD_ROWS
    gain_rows = []
    for j in range(HALF):
        there = fixed(j)
        gain = gain_ref[pl.ds(core * HALF + j, 1), :]
        before = before_ref[j]
        pair, gain_row = 0.0, 0.0
        for b in range(CORES):
            state = jnp.where(core != b, before + first_ref[j], before).astype(BF16)
            state_ref[b, j] = state
            q, grad_f = in_ref[b, 0, :, there], in_ref[b, 3, :, there].astype(F32)
            output = loc_ref[b, :, there] + dot(q, state, 1, 0)
            center = output - jnp.mean(output, axis=-1, keepdims=True)
            inv_std = lax.rsqrt(jnp.mean(center * center, axis=-1, keepdims=True) + NORM_EPS)
            normed = center * inv_std
            scaled = grad_f * gain
            d_out = inv_std * (
                scaled
                - jnp.mean(scaled, axis=-1, keepdims=True)
                - normed * jnp.mean(scaled * normed, axis=-1, keepdims=True)
            )
            dout = d_out.astype(BF16)
            dout_ref[b, :, there] = dout
            pair = pair + dot(q, dout, 0, 0)
            gain_row = gain_row + jnp.sum(grad_f * normed, axis=0, keepdims=True)
        for i in range(slices):
            pay_ref[j * slices + i, :rows] = pair[i * rows : (i + 1) * rows]
        gain_rows.append(gain_row)
    grads = jnp.concatenate(gain_rows + [bias_ref[...]], axis=0)
    for s in range(pay_ref.shape[0]):
        pay_ref[s, rows:] = grads


def near_kernel(
    core_ref, in_ref, dout_ref, state_ref, gain_ref, bias_ref, first_ref, second_ref,
    gq_ref, gk_ref, gv_ref, send_ref, own_ref, other_ref, pack_ref,
):
    core = core_ref[0]
    for p, ref in enumerate((gain_ref, bias_ref)):
        pack_ref[0, p * HALF : (p + 1) * HALF] = ref[pl.ds(core * HALF, HALF), :]
        for j in range(HALF):
            at, row = cols(core * HALF + j), p * HALF + j
            pack_ref[1, row : row + 1] = first_ref[p : p + 1, at]
            pack_ref[2, row : row + 1] = second_ref[p : p + 1, at]
    causal = causal_mask()
    for j in range(HALF):
        there = fixed(j)
        for b in range(CORES):
            q, k, v = (in_ref[b, i, :, there] for i in range(3))
            dout = dout_ref[b, :, there]
            (own_ref, other_ref)[b][j] = dot(q, dout, 0, 0)
            w = jnp.where(causal, dot(q, k, 1, 1), 0.0).astype(BF16)
            gw = jnp.where(causal, dot(dout, v, 1, 1), 0.0).astype(BF16)
            gq = dot(gw, k, 1, 0) + dot(dout, state_ref[b, j], 1, 1)
            gk = dot(gw, q, 0, 0)
            gv = dot(w, dout, 0, 0)
            if b == 0:
                gq_ref[:, there], gk_ref[:, there], gv_ref[:, there] = gq.astype(BF16), gk, gv
            else:
                send_ref[0, :, there], send_ref[1, :, there], send_ref[2, :, there] = gq, gk, gv


def half_at(half):
    return pl.ds(pl.multiple_of(half * HALF_WIDTH, HALF_WIDTH), HALF_WIDTH)


def join_kernel(core_ref, own_ref, recv_ref, out_ref):
    core = core_ref[0]
    out_ref[:, half_at(core)] = own_ref[...]
    out_ref[:, half_at(1 - core)] = recv_ref[0].astype(BF16)


def lamb_direction(weight, grad, first, second):
    first_new = BETA_ONE * first + (1.0 - BETA_ONE) * grad
    second_new = BETA_TWO * second + (1.0 - BETA_TWO) * grad * grad
    return (
        first_new / CORRECT_ONE / (jnp.sqrt(second_new / CORRECT_TWO) + ADAM_EPS)
        + DECAY_RATE * weight
    )


def whole_sum(x):
    return jnp.sum(jnp.sum(x, axis=1, keepdims=True), axis=0, keepdims=True)


def step_kernel(grads_ref, pack_ref, step_ref, squares_ref):
    for i in range(2):
        at = slice(i * HALF, (i + 1) * HALF)
        weight = pack_ref[0, at]
        step = lamb_direction(weight, grads_ref[at], pack_ref[1, at], pack_ref[2, at])
        step_ref[at] = step
        for row, sum_of in ((i, whole_sum(weight * weight)), (2 + i, whole_sum(step * step))):
            squares_ref[row : row + 1] = jnp.broadcast_to(sum_of, (1, HEAD_DIM))
    squares_ref[4:8] = jnp.zeros((4, HEAD_DIM), F32)


def pack_kernel(core_ref, after_ref, own_ref, step_ref, squares_ref, out_ref):
    core = core_ref[0]
    for j in range(HALF):
        after = after_ref[j]
        out_ref[j * HEAD_DIM : (j + 1) * HEAD_DIM] = jnp.where(core == 1, after + own_ref[j], after)
    out_ref[STEP_ROW : STEP_ROW + 8] = step_ref[...]
    out_ref[STEP_ROW + 8 :] = squares_ref[...]


def far_kernel(
    core_ref, k_ref, v_ref, gk_own_ref, gv_own_ref, recv_ref, after_ref, other_ref, far_ref, step_ref, squares_ref,
    gain_ref, bias_ref, gk_ref, gv_ref, new_gain_ref, new_bias_ref,
):
    core = core_ref[0]
    for j in range(HALF):
        there = fixed(j)
        for b in range(CORES):
            if b == 0:
                at = cols(core * HALF + j)
                after = after_ref[j]
                later = jnp.where(core == 0, after + other_ref[j], after).astype(BF16)
                gk, gv = gk_own_ref[:, there], gv_own_ref[:, there]
            else:
                at = cols((1 - core) * HALF + j)
                later = far_ref[there].astype(BF16)
                gk, gv = recv_ref[1, :, there], recv_ref[2, :, there]
            gk_ref[:, at] = (gk + dot(v_ref[:, at], later, 1, 1)).astype(BF16)
            gv_ref[:, at] = (gv + dot(k_ref[:, at], later, 1, 0)).astype(BF16)
    squares = squares_ref[...] + far_ref[STEP_ROW + 8 :]
    for i, (weight_ref, out) in enumerate(((gain_ref, new_gain_ref), (bias_ref, new_bias_ref))):
        ratio = jnp.sqrt(squares[i : i + 1]) / jnp.sqrt(squares[2 + i : 3 + i] + TRUST_EPS)
        steps = (step_ref[i * HALF : (i + 1) * HALF], far_ref[STEP_ROW + i * HALF : STEP_ROW + (i + 1) * HALF])
        for half, step in zip((core, 1 - core), steps):
            at = pl.ds(half * HALF, HALF)
            out[at, :] = weight_ref[at, :] - LEARN_RATE * ratio * step


def call(kernel, outs, *args, scalar=True):
    vmem = pl.BlockSpec(memory_space=pltpu.VMEM)
    specs = [vmem] * len(args)
    if scalar:
        specs[0] = pl.BlockSpec(memory_space=pltpu.SMEM)
    return pl.pallas_call(
        kernel,
        out_shape=[jax.ShapeDtypeStruct(s, d) for s, d in outs],
        in_specs=specs,
        out_specs=[vmem] * len(outs),
        compiler_params=pltpu.CompilerParams(vmem_limit_bytes=VMEM_LIMIT),
    )(*args)


STATE = (HALF, HEAD_DIM, HEAD_DIM)


def swap(array, axis="core", step=1):
    n = lax.axis_size(axis)
    return lax.ppermute(array, axis, [(i, i ^ step) for i in range(n)])


def group_swap(array, steps):
    pairs = [(h * CORES + c, (h ^ steps[c]) * CORES + c) for h in range(GROUP) for c in range(CORES)]
    return lax.ppermute(array, ("h", "core"), pairs)


def exchange(array, axis):
    return lax.all_to_all(array, axis, 0, 0, tiled=True)


NEAR = ("y", "l")


def chip_scan(pay, reverse, beside_one, beside_two, given):
    members = GROUP * GROUP
    rows = HALF * HEAD_DIM // members
    extra = pay.shape[1] - rows
    part = (members, rows, HEAD_DIM)
    at_s = lax.axis_index(("h", "core")).astype(jnp.int32).reshape(1)
    landed = exchange(pay, NEAR)
    if reverse:
        landed, given = lax.optimization_barrier((landed, given))
    sums_shape = (GROUP * rows + extra, HEAD_DIM)
    part_sums, send = call(
        functools.partial(group_kernel, reverse, rows), [(part, F32), (sums_shape, F32)], landed, scalar=False
    )
    near, given = lax.optimization_barrier((group_swap(send, (1, 3)), beside_one(given)))
    (both,) = call(functools.partial(sum_kernel, reverse, rows), [(sums_shape, F32)], at_s, send, near)
    far, made = lax.optimization_barrier((group_swap(both, (3, 1)), beside_two(given)))
    outs = [(part, F32)] + ([((extra, HEAD_DIM), F32)] if extra else [])
    sums, *rest = call(functools.partial(offset_kernel, reverse, rows), outs, at_s, near, far, both, part_sums)
    return exchange(sums, NEAR).reshape(STATE), rest, made


def per_device(queries, keys, values, grad_out, norm_gain, norm_bias, first_moment, second_moment):
    rows, width = queries.shape
    half = (rows, HALF_WIDTH)
    members = GROUP * GROUP
    slice_rows = HALF * HEAD_DIM // members
    core_s = lax.axis_index("core").astype(jnp.int32).reshape(1)
    by_head = (HEADS_HERE, HEAD_DIM)
    gain, bias = norm_gain.reshape(by_head), norm_bias.reshape(by_head)

    def share_inputs():
        (wide,) = call(widen_kernel, [((4,) + half, F32)], core_s, queries, keys, values, grad_out)
        return swap(wide)

    def local_part(recv):
        return call(
            local_kernel, [((CORES, 4) + half, BF16), ((CORES,) + half, F32), (STATE, F32), ((HALF, HEAD_DIM), F32)],
            core_s, queries, keys, values, grad_out, recv,
        )

    def near_grads(both, dout, state):
        return call(
            near_kernel,
            [(half, BF16), (half, F32), (half, F32), ((3,) + half, F32), (STATE, F32), (STATE, F32), ((3,) + by_head, F32)],
            core_s, both, dout, state, gain, bias, first_moment, second_moment,
        )

    def share_grads(gq_own, gk_own, gv_own, send, own, other, pack):
        near = swap(send)
        (grad_q,) = call(join_kernel, [((rows, width), BF16)], core_s, gq_own, near)
        return grad_q, gk_own, gv_own, near, own, other, pack

    mine, send = call(pair_kernel, [(STATE, F32)] * 2, core_s, jnp.stack([keys, values]))
    (pay,) = call(add_kernel, [((members, slice_rows, HEAD_DIM), F32)], mine, swap(send), scalar=False)
    before, _, (both, local, first_state, bias_sums) = chip_scan(pay, False, lambda recv: recv, local_part, share_inputs())

    pay_shape = (members, slice_rows + GRAD_ROWS, HEAD_DIM)
    state, dout, pay = call(
        norm_kernel,
        [((CORES,) + STATE, BF16), ((CORES,) + half, BF16), (pay_shape, F32)],
        core_s, both, gain, local, before, first_state, bias_sums,
    )
    after, (grads,), (grad_q, gk_own, gv_own, near, own, other, pack) = chip_scan(
        pay, True, lambda tied: near_grads(*tied), lambda tied: share_grads(*tied), (both, dout, state)
    )

    step, squares = call(step_kernel, [(by_head, F32)] * 2, grads, pack, scalar=False)
    after, squares = lax.optimization_barrier((after, lax.psum(squares, "fsdp")))
    (send,) = call(pack_kernel, [((STEP_ROW + 16, HEAD_DIM), F32)], core_s, after, own, step, squares)
    far = swap(send)
    grad_k, grad_v, new_gain, new_bias = call(
        far_kernel, [((rows, width), BF16)] * 2 + [(by_head, F32)] * 2,
        core_s, keys, values, gk_own, gv_own, near, after, other, far, step, squares, gain, bias,
    )
    return grad_q, grad_k, grad_v, new_gain.reshape(width), new_bias.reshape(width)


def solution(mesh):
    seq, fsdp = mesh.devices.shape
    fine = Mesh(
        mesh.devices.reshape(GROUP, seq // (GROUP * GROUP * CORES), GROUP, CORES, fsdp), ("y", "h", "l", "core", "fsdp")
    )
    big = P(("y", "h", "l", "core"), "fsdp")
    return jax.shard_map(
        per_device,
        mesh=fine,
        in_specs=(big, big, big, big, P("fsdp"), P("fsdp"), P(None, "fsdp"), P(None, "fsdp")),
        out_specs=(big, big, big, P("fsdp"), P("fsdp")),
        check_vma=False,
    )
```
